32 devices in a mesh: slab: 16 (over z, y, core), sub: 2 (over x).
Axes of the slice: x: 2, y: 2, z: 4, core: 2. Of those that a mesh axis runs over, the one named last changes fastest.
Arguments:
- rhs_interior: float32 [16, 8, 2, 256, 128], P('slab', 'sub'), may hold values from -6 to 6
- rhs_separator: float32 [16, 2, 512, 128], P('slab'), may hold values from -6 to 6
- inverse_blocks: float32 [16, 8, 2, 256, 256], P('slab', 'sub'), may hold values from -0.375 to 0.375
- coupling: float32 [16, 8, 2, 512, 256], P('slab', 'sub'), may hold values from -0.0625 to 0.0625
- separator_rows: int32 [16, 8, 512], P('slab', 'sub'), may hold values from 0 to 511, each once within a row
- separator_inverse: float32 [16, 2, 512, 512], P('slab'), may hold values from -1.1 to 1.1
- transfer: float32 [16, 2, 512, 512], P('slab'), may hold values from -1.1 to 1.1
Outputs:
- interior_solution: float32 [16, 8, 2, 256, 128], P('slab', 'sub')
- separator_solution: float32 [16, 2, 512, 128], P('slab')
The draws below stay inside these ranges and needn't reach their ends.
Inputs may be any that keep to these rules, and one draw needn't show every extreme that they name: Each block's separator_rows lists every separator row 0 to 511 exactly once.
All inputs are finite; a program needn't handle non-finite values.
Results may differ from the reference program's by a relative error of at most 0.0003.
Values sent between devices are 32-bit elements; how exact they have to be, the bound alone decides.
No kernel may reach another device: no remote copies, remote signals or barrier semaphores. Data moves between devices by JAX's collectives and lax.ppermute only.
A program may use at most 128 MiB of HBM per device.

```python
import math
import jax
import jax.numpy as jnp
from jax import lax

M = 256
TRACE_UNKNOWNS = 512
SHOTS = 128
NB = 4
NBLK = 8
SLAB_COUNT = 16


def draw_separator_inverse(key, part):
    first, second = jax.random.split(jax.random.fold_in(key, 11))
    noise = jax.random.normal(first, (SLAB_COUNT, 2, TRACE_UNKNOWNS, TRACE_UNKNOWNS), jnp.float32)
    noise = jnp.clip(noise, -5.0, 5.0) * (0.5 / math.sqrt(TRACE_UNKNOWNS))
    diagonal = jax.random.uniform(second, (SLAB_COUNT, 1, TRACE_UNKNOWNS), jnp.float32, 0.35, 0.6)
    eye = jnp.eye(TRACE_UNKNOWNS, dtype=jnp.float32)
    real_mask = jnp.array([1.0, 0.0], jnp.float32)[None, :, None, None]
    return noise + real_mask * eye[None, None] * diagonal[..., None, :]


def draw_transfer(key, part):
    random_keys = jax.random.split(jax.random.fold_in(key, 23), 4)
    absolute_size = jnp.exp(jax.random.uniform(random_keys[0], (SLAB_COUNT, TRACE_UNKNOWNS), jnp.float32, math.log(0.3), math.log(0.97)))
    pulse_batch = jax.random.bernoulli(random_keys[1], 3.0 / SLAB_COUNT, (SLAB_COUNT, TRACE_UNKNOWNS))
    absolute_size = absolute_size * jnp.where(pulse_batch, 0.6, 1.0)
    phase = jax.random.uniform(random_keys[2], (SLAB_COUNT, TRACE_UNKNOWNS), jnp.float32, -math.pi, math.pi)
    noise = jnp.clip(jax.random.normal(random_keys[3], (SLAB_COUNT, 2, TRACE_UNKNOWNS, TRACE_UNKNOWNS), jnp.float32), -5.0, 5.0) * (0.2 / math.sqrt(2 * TRACE_UNKNOWNS))
    eye = jnp.eye(TRACE_UNKNOWNS, dtype=jnp.float32)
    diagonal = jnp.stack([absolute_size * jnp.cos(phase), absolute_size * jnp.sin(phase)], axis=1)
    return noise + eye[None, None] * diagonal[..., None, :]


def level_of(own_key, dims, cuts, low, high):
    level = 1.0
    for dim, blocks in cuts:
        heights = jax.random.uniform(jax.random.fold_in(jax.random.fold_in(own_key, 6), dim), (blocks,), jnp.float32, low / len(cuts), high / len(cuts))
        level = level * jnp.repeat(jnp.exp(heights), dims[dim] // blocks).reshape((-1,) + (1,) * (len(dims) - 1 - dim))
    return level


def scatter_about(rng, dims, scale, limit, shards=(), kind=jnp.bfloat16):
    values = jax.random.normal(rng, dims, jnp.float32) * scale
    if len(shards) > 0:
        values = level_of(rng, dims, shards, -0.22, 0.18) * values
    return jnp.clip(values, min=-limit, max=limit).astype(kind)


def setup_inputs(seed: int = 0) -> dict:
    splits = jax.random.split(jax.random.key(seed), 8)
    return {
        "rhs_interior": scatter_about(splits[0], (SLAB_COUNT, NBLK, 2, M, SHOTS), 1.0, 6.0, ((0, 16), (1, 2)), jnp.float32),
        "rhs_separator": scatter_about(splits[1], (SLAB_COUNT, 2, TRACE_UNKNOWNS, SHOTS), 1.0, 6.0, ((0, 16),), jnp.float32),
        "inverse_blocks": scatter_about(splits[2], (SLAB_COUNT, NBLK, 2, M, M), M ** -0.5, 0.375, ((0, 16), (1, 2)), jnp.float32),
        "coupling": scatter_about(splits[3], (SLAB_COUNT, NBLK, 2, TRACE_UNKNOWNS, M), (4 * TRACE_UNKNOWNS * NB) ** -0.5, 0.0625, ((0, 16), (1, 2)), jnp.float32),
        "separator_rows": jax.vmap(lambda own: jax.random.permutation(own, TRACE_UNKNOWNS))(jax.random.split(splits[4], SLAB_COUNT * NBLK)).reshape((SLAB_COUNT, NBLK, TRACE_UNKNOWNS)).astype(jnp.int32),
        "separator_inverse": draw_separator_inverse(jax.random.fold_in(splits[7], 71), 0),
        "transfer": draw_transfer(jax.random.fold_in(splits[7], 71), 0),
    }


HIGH = lax.Precision.HIGHEST


def multiply(left, right):
    return jnp.matmul(left, right, precision=HIGH)


def complex_product(left, right):
    real_part = multiply(left[..., 0, :, :], right[..., 0, :, :]) - multiply(left[..., 1, :, :], right[..., 1, :, :])
    imag_part = multiply(left[..., 0, :, :], right[..., 1, :, :]) + multiply(left[..., 1, :, :], right[..., 0, :, :])
    return jnp.stack([real_part, imag_part], axis=-3)


def flipped(matrix):
    return jnp.swapaxes(matrix, -1, -2)


def placed_coupling(weights, rows):
    count = rows.shape[-1]
    spread = (rows[:, None, :] == jnp.arange(count)[None, :, None]).astype(weights.dtype)
    return jnp.einsum("bpr,bcrm->bcpm", spread, weights, precision=HIGH)


def reference(rhs_interior, rhs_separator, inverse_blocks, coupling, separator_rows, separator_inverse, transfer):
    def slab_sum(items):
        loads, lower, weights, rows = items
        placed = placed_coupling(weights, rows)
        return jnp.sum(complex_product(placed, complex_product(lower, loads)), axis=0)

    sums = lax.map(slab_sum, (rhs_interior, inverse_blocks, coupling, separator_rows))
    local = complex_product(separator_inverse, rhs_separator - sums)
    traces = []
    incoming = jnp.zeros_like(local[0])
    for index in range(SLAB_COUNT):
        incoming = local[index] - complex_product(transfer[index], incoming)
        traces.append(incoming)
    finished_slabs = [None] * SLAB_COUNT
    carried = jnp.zeros_like(local[0])
    for index in reversed(range(SLAB_COUNT)):
        value = traces[index] - carried
        finished_slabs[index] = value
        carried = complex_product(flipped(transfer[index]), value)
    finished_slabs = jnp.stack(finished_slabs)

    def slab_solution(items):
        loads, lower, weights, rows, value = items
        placed = placed_coupling(weights, rows)
        eliminated = complex_product(lower, loads)
        return complex_product(flipped(lower), eliminated - complex_product(flipped(placed), value[None]))

    interior = lax.map(slab_solution, (rhs_interior, inverse_blocks, coupling, separator_rows, finished_slabs))
    return interior, finished_slabs
```

```python
import jax
import jax.numpy as jnp
from jax import lax
from jax.experimental import pallas as pl
from jax.experimental.pallas import tpu as pltpu
from jax.sharding import PartitionSpec as P

NEAR = lax.Precision.HIGH
GROUP = 4
CHUNKS = 4
MIB = 1 << 20


def move(value, target):
    slabs, subs = lax.axis_size("slab"), lax.axis_size("sub")
    pairs = []
    for slab in range(slabs):
        for sub in range(subs):
            goal = target(slab, sub)
            if goal is not None:
                pairs.append((slab * subs + sub, goal[0] * subs + goal[1]))
    return lax.ppermute(value, ("slab", "sub"), pairs)


def swap(value, mask):
    return move(value, lambda slab, sub: (slab ^ mask, sub))


def shift_sub(value, steps):
    subs = lax.axis_size("sub")
    return move(value, lambda slab, sub: (slab, (sub + steps) % subs))


def pick(array, index):
    return lax.dynamic_index_in_dim(array, index, 0, keepdims=False)


def near_product(spec, left, right):
    def term(a, b):
        return jnp.einsum(spec, left[:, a], right[:, b], precision=NEAR)

    return jnp.stack([term(0, 0) - term(1, 1), term(0, 1) + term(1, 0)], axis=1)


def split(value):
    high = value.astype(jnp.bfloat16)
    return high, (value - high.astype(jnp.float32)).astype(jnp.bfloat16)


def dot(left, right):
    return jnp.dot(left, right, preferred_element_type=jnp.float32)


def dot_flipped(left, right):
    return lax.dot_general(left, right, (((1,), (1,)), ((), ())), preferred_element_type=jnp.float32)


def row_product(rows, matrix, slot, product):
    half = rows.shape[0] // 2
    size = rows.shape[1]
    high, low = split(rows)
    both = jnp.concatenate([high, low], axis=0)

    def against(start):
        wide = product(both, matrix[slot, 0, start : start + size])
        return wide[: 2 * half] + wide[2 * half :] + product(high, matrix[slot, 1, start : start + size])

    real, imag = against(0), against(size)
    return real + jnp.concatenate([-imag[half:], imag[:half]], axis=0)


def whole():
    return pl.BlockSpec(memory_space=pltpu.VMEM)


def gathered_blocks(transfer):
    subs = lax.axis_size("sub")
    part = lax.axis_index("sub")
    size = transfer.shape[-1]
    own = transfer.reshape(2 * size, size)
    rows = 2 * size // subs
    step = rows // CHUNKS
    mine = lax.dynamic_slice_in_dim(own, part * rows, rows, 0)
    crossed = [swap(mine[c * step : (c + 1) * step], 2) for c in range(CHUNKS)]
    near = swap(own, 1)
    pieces = []
    for c in range(CHUNKS):
        for k in range(subs):
            pieces.append((c, k, shift_sub(crossed[c], k) if k else crossed[c]))
    far = [swap(piece, 1) for _, _, piece in pieces]

    def kernel(own_ref, near_ref, *refs):
        piece_refs, far_refs, out = refs[: len(pieces)], refs[len(pieces) : -1], refs[-1]
        here = lax.axis_index("sub")

        def put(slot, start, value):
            count = value.shape[0]
            out[slot, 0, pl.ds(start, count)], out[slot, 1, pl.ds(start, count)] = split(value)

        put(0, 0, own_ref[...])
        put(1, 0, near_ref[...])
        for (c, k, _), near_piece, far_piece in zip(pieces, piece_refs, far_refs):
            start = pl.multiple_of(lax.rem(here - k + subs, subs) * rows + c * step, step)
            put(2, start, near_piece[...])
            put(3, start, far_piece[...])

    return pl.pallas_call(
        kernel,
        out_shape=pltpu.VMEM((GROUP, 2, 2 * size, size), jnp.bfloat16),
        in_specs=[whole()] * (2 + 2 * len(pieces)),
        out_specs=whole(),
        compiler_params=pltpu.CompilerParams(vmem_limit_bytes=32 * MIB),
        name="split_blocks",
    )(own, near, *[piece for _, _, piece in pieces], *far)


def turn(state, incoming, blocks, group, forward, backward):
    shape = state.shape[1:]

    def kernel(*refs):
        if incoming is None:
            state_in, block_ref, state_out, answer, carry = refs
        else:
            state_in, incoming_ref, block_ref, state_out, answer, carry = refs
        position = lax.axis_index("slab")
        member = lax.rem(position, GROUP)

        @pl.when(lax.div(position, GROUP) == group)
        def _():
            value = None if incoming is None else incoming_ref[...]
            if forward:
                for i in range(GROUP):
                    slot = member ^ i
                    local = state_in[slot]
                    if value is None:
                        value = local
                    else:
                        value = local - row_product(value, block_ref, slot, dot_flipped)
                    state_out[slot] = value
                carry[...] = value
            if backward:
                value = None if forward else value
                for i in reversed(range(GROUP)):
                    slot = member ^ i
                    trace = state_out[slot] if forward else state_in[slot]
                    value = trace if value is None else trace - value
                    answer[i] = value
                    value = row_product(value, block_ref, slot, dot)
                carry[...] = value

    operands = (state, blocks) if incoming is None else (state, incoming, blocks)
    return pl.pallas_call(
        kernel,
        out_shape=(
            jax.ShapeDtypeStruct(state.shape, jnp.float32),
            jax.ShapeDtypeStruct(state.shape, jnp.float32),
            jax.ShapeDtypeStruct(shape, jnp.float32),
        ),
        in_specs=[whole()] * len(operands),
        out_specs=(whole(), whole(), whole()),
        input_output_aliases={0: 0},
        compiler_params=pltpu.CompilerParams(vmem_limit_bytes=16 * MIB),
        name="sweep_turn",
    )(*operands)


def body(
    rhs_interior,
    rhs_separator,
    inverse_blocks,
    coupling,
    separator_rows,
    separator_inverse,
    transfer,
):
    slabs, subs = lax.axis_size("slab"), lax.axis_size("sub")
    part = lax.axis_index("sub")
    member = lax.rem(lax.axis_index("slab"), GROUP)
    turns = slabs // GROUP
    loads, lower, weights, rows = rhs_interior[0], inverse_blocks[0], coupling[0], separator_rows[0]
    size, shots = rhs_separator.shape[-2:]
    wide = shots // subs
    width = wide // GROUP

    blocks = gathered_blocks(transfer[0])

    spread = (rows[:, None, :] == jnp.arange(size)[None, :, None]).astype(jnp.float32)
    eliminated = near_product("bij,bjn->bin", lower, loads)
    coupled = near_product("bij,bjn->bin", weights, eliminated)
    load = jnp.einsum("bpr,bcrn->cpn", spread, coupled, precision=NEAR)
    load = load.reshape(2, size, subs, wide).transpose(2, 0, 1, 3)
    right = pick(rhs_separator[0].reshape(2, size, subs, wide).transpose(2, 0, 1, 3), part)
    right = right - pick(load, part)
    for k in range(1, subs):
        right = right - shift_sub(pick(load, lax.rem(part + k, subs)), k)
    local = near_product("bij,bjn->bni", separator_inverse, right[None])[0]
    local = local.reshape(2, GROUP, width, size).transpose(1, 0, 2, 3).reshape(GROUP, 2 * width, size)
    state = [pick(local, member)]
    for j in range(1, GROUP):
        state.append(swap(pick(local, member ^ j), j))
    state = jnp.stack(state)

    joined = near_product("bij,bjk->bik", weights, lower)
    joined = jnp.einsum("bpr,bcrk->bcpk", spread, joined, precision=NEAR)
    plain = near_product("bji,bjn->bin", lower, eliminated)

    def hop(value, source, steps):
        return move(
            value,
            lambda slab, sub: (slab + GROUP * steps, sub) if slab // GROUP == source else None,
        )

    incoming = None
    for group in range(turns - 1):
        state, answer, carry = turn(state, incoming, blocks, group, True, False)
        incoming = hop(carry, group, 1)
    state, answer, carry = turn(state, incoming, blocks, turns - 1, True, True)
    answers = answer
    here = lax.div(lax.axis_index("slab"), GROUP)
    for group in reversed(range(turns - 1)):
        incoming = hop(carry, group + 1, -1)
        state, answer, carry = turn(state, incoming, blocks, group, False, True)
        answers = jnp.where(here == group, answer, answers)

    groups = [
        [(g * GROUP + m) * subs + u for m in range(GROUP) for u in range(subs)] for g in range(turns)
    ]
    outgoing = jnp.broadcast_to(answers[:, None], (GROUP, subs) + answers.shape[1:])
    outgoing = outgoing.reshape((GROUP * subs,) + answers.shape[1:])
    arrived = lax.all_to_all(
        outgoing, ("slab", "sub"), 0, 0, axis_index_groups=groups, tiled=True
    )
    solved = arrived.reshape(GROUP, subs, 2, width, size).transpose(2, 1, 0, 3, 4)
    solved = solved.reshape(2, shots, size)
    count = joined.shape[0]
    taken = near_product(
        "bpk,bnp->bkn", joined, jnp.broadcast_to(solved[None], (count,) + solved.shape)
    )
    return ((plain - taken)[None], jnp.swapaxes(solved, 1, 2)[None])


def solution(mesh):
    in_specs = (
        P("slab", "sub", None, None, None),
        P("slab", None, None, None),
        P("slab", "sub", None, None, None),
        P("slab", "sub", None, None, None),
        P("slab", "sub", None),
        P("slab", None, None, None),
        P("slab", None, None, None),
    )
    out_specs = (P("slab", "sub", None, None, None), P("slab", None, None, None))
    return jax.shard_map(body, mesh=mesh, in_specs=in_specs, out_specs=out_specs, check_vma=False)
```

```python
import jax
import jax.numpy as jnp
from jax import lax
from jax.experimental import pallas as pl
from jax.experimental.pallas import tpu as pltpu
from jax.sharding import PartitionSpec as P

GROUP = 4
RELAYED = 1
DIRECT = 1
AHEAD = 2
MIB = 1 << 20
LIGHT = pl.CostEstimate(flops=1, bytes_accessed=1, transcendentals=0)


def move(value, target):
    slabs, subs = lax.axis_size("slab"), lax.axis_size("sub")
    pairs = []
    for slab in range(slabs):
        for sub in range(subs):
            goal = target(slab, sub)
            if goal is not None:
                pairs.append((slab * subs + sub, goal[0] * subs + goal[1]))
    return lax.ppermute(value, ("slab", "sub"), pairs)


def swap(value, mask):
    return move(value, lambda slab, sub: (slab ^ mask, sub))


def shift_sub(value, steps):
    subs = lax.axis_size("sub")
    return move(value, lambda slab, sub: (slab, (sub + steps) % subs))


def pick(array, index):
    return lax.dynamic_index_in_dim(array, index, 0, keepdims=False)


def split(value):
    high = value.astype(jnp.bfloat16)
    return high, (value - high.astype(jnp.float32)).astype(jnp.bfloat16)


def dot(left, right):
    return jnp.dot(left, right, preferred_element_type=jnp.float32)


def dot_flipped(left, right):
    return lax.dot_general(left, right, (((1,), (1,)), ((), ())), preferred_element_type=jnp.float32)


def row_product(rows, matrix, slot, product):
    half = rows.shape[0] // 2
    size = rows.shape[1]
    high, low = split(rows)
    both = jnp.concatenate([high, low], axis=0)

    def against(start):
        wide = product(both, matrix[slot, 0, start : start + size])
        return wide[: 2 * half] + wide[2 * half :] + product(high, matrix[slot, 1, start : start + size])

    real, imag = against(0), against(size)
    return real + jnp.concatenate([-imag[half:], imag[:half]], axis=0)


def whole():
    return pl.BlockSpec(memory_space=pltpu.VMEM)


def plan(size, subs):
    step = 5 * size // 4 // RELAYED // subs
    direct = (2 * size - RELAYED * step * subs) // DIRECT
    return step, direct


def crossed_blocks(own, near):
    subs = lax.axis_size("sub")
    part = lax.axis_index("sub")
    step, direct = plan(own.shape[1], subs)
    shares = [
        lax.dynamic_slice_in_dim(own, (c * subs + part) * step, step, 0) for c in range(RELAYED)
    ]
    crossed = [swap(share, 2) for share in shares]
    start = RELAYED * subs * step
    for c in range(DIRECT):
        share, near = lax.optimization_barrier((own[start + c * direct : start + (c + 1) * direct], near))
        crossed.append(swap(share, 2))
    return crossed, near


def relayed_pieces(c, chunk):
    subs = lax.axis_size("sub")
    now = [chunk] + [shift_sub(chunk, k) for k in range(1, subs)]
    return [(c, k, piece) for k, piece in enumerate(now)]


def in_hbm(value):
    return pltpu.with_memory_space_constraint(value, pltpu.HBM)


def split_blocks(own, near, pieces, far, terms):
    subs = lax.axis_size("sub")
    size = own.shape[1]
    step, direct = plan(size, subs)
    values = [own, near] + [piece for _, _, piece in pieces] + list(far)
    count = len(pieces)

    def kernel(*refs):
        sources, (terms_ref, out, state) = refs[: len(values)], refs[len(values) : len(values) + 3]
        here = lax.axis_index("sub")
        member = lax.rem(lax.axis_index("slab"), GROUP)
        for slot in range(GROUP):
            value = terms_ref[(member ^ slot) * subs]
            for sub in range(1, subs):
                value = value + terms_ref[(member ^ slot) * subs + sub]
            state[slot] = value
        for i, source in enumerate(sources):
            if i < 2:
                out[i, 0], out[i, 1] = split(source[...])
                continue
            slot, (c, k, _) = 2 + (i - 2) // count, pieces[(i - 2) % count]
            if c < RELAYED:
                start = pl.multiple_of((c * subs + lax.rem(here - k + subs, subs)) * step, step)
                rows = pl.ds(start, step)
            else:
                start = RELAYED * subs * step + (c - RELAYED) * direct
                rows = pl.ds(start, direct)
            out[slot, 0, rows], out[slot, 1, rows] = split(source[...])

    return pl.pallas_call(
        kernel,
        out_shape=(
            pltpu.VMEM((GROUP, 2, 2 * size, size), jnp.bfloat16),
            jax.ShapeDtypeStruct((GROUP,) + terms.shape[1:], jnp.float32),
        ),
        in_specs=[whole()] * (len(values) + 1),
        out_specs=(whole(), whole()),
        compiler_params=pltpu.CompilerParams(vmem_limit_bytes=16 * MIB),
        name="split_blocks",
    )(*values, terms)


def near_dot(left, right):
    return dot(left[0], right[0]) + (dot(left[0], right[1]) + dot(left[1], right[0]))


def column_product(matrix, columns):
    half = columns.shape[1] // 2
    columns = split(columns)
    real = near_dot(split(matrix[0]), columns)
    imag = near_dot(split(matrix[1]), columns)
    return jnp.concatenate(
        [real[:, :half] - imag[:, half:], real[:, half:] + imag[:, :half]], axis=1
    )


def side_by_side(pair):
    return jnp.concatenate([pair[0], pair[1]], axis=1)


def spread_of(rows):
    count = rows.shape[1]
    place = lax.broadcasted_iota(jnp.int32, (count, count), 0)
    return jnp.where(rows == place, 1.0, 0.0).astype(jnp.bfloat16)


def spread_product(spread, columns):
    high, low = split(columns)
    return dot(spread, high) + dot(spread, low)


def separator_part(loads, lower, weights, rows, right, inverse):
    count, _, inner, shots = loads.shape
    size = right.shape[1]
    subs = lax.axis_size("sub")
    width = shots // (subs * GROUP)

    def kernel(load_hbm, lower_hbm, weight_hbm, rows_hbm, right_hbm, inverse_hbm, out, eliminated_hbm, *scratch):
        load_ref, lower_ref, weight_ref, right_ref, inverse_ref = scratch[:5]
        eliminated_ref, total, spread, rows_ref, arrived, right_arrived, inverse_arrived, rows_arrived, left = scratch[5:]

        def copies(b):
            sources = (load_hbm, lower_hbm, weight_hbm)
            rooms = (load_ref, lower_ref, weight_ref)
            return [
                pltpu.make_async_copy(source.at[b], room.at[b], arrived.at[i, b])
                for i, (source, room) in enumerate(zip(sources, rooms))
            ]

        def leaving(b):
            return pltpu.make_async_copy(eliminated_ref.at[b], eliminated_hbm.at[b], left.at[b])

        right_copy = pltpu.make_async_copy(right_hbm, right_ref, right_arrived)
        inverse_copy = pltpu.make_async_copy(inverse_hbm, inverse_ref, inverse_arrived)
        rows_copy = pltpu.make_async_copy(rows_hbm, rows_ref, rows_arrived)
        rows_copy.start()
        for b in range(min(AHEAD, count)):
            for copy in copies(b):
                copy.start()
        rows_copy.wait()
        for b in range(count):
            spread[b] = spread_of(rows_ref[b : b + 1])
        for b in range(count):
            for copy in copies(b):
                copy.wait()
            if b + AHEAD < count:
                for copy in copies(b + AHEAD):
                    copy.start()
            elif b + AHEAD == count:
                right_copy.start()
                inverse_copy.start()
            eliminated = column_product(lower_ref.at[b], side_by_side(load_ref.at[b]))
            eliminated_ref[b] = eliminated.T
            leaving(b).start()
            coupled = column_product(weight_ref.at[b], eliminated)
            load = spread_product(spread[b], coupled)
            total[...] = total[...] + load if b else load

        right_copy.wait()
        inverse_copy.wait()
        kept = jnp.where(lax.axis_index("sub") == 0, side_by_side(right_ref), 0.0)
        local = column_product(inverse_ref, kept - total[...])
        for half in range(2):
            shot_rows = local[:, half * shots : (half + 1) * shots].T
            for sub in range(subs):
                for member in range(GROUP):
                    start = (sub * GROUP + member) * width
                    out[member * subs + sub, half * width : (half + 1) * width] = shot_rows[
                        start : start + width
                    ]
        for b in range(count):
            leaving(b).wait()

    hbm = pl.BlockSpec(memory_space=pltpu.HBM)
    return pl.pallas_call(
        kernel,
        out_shape=(
            jax.ShapeDtypeStruct((GROUP * subs, 2 * width, size), jnp.float32),
            pltpu.HBM((count, 2 * shots, inner), jnp.float32),
        ),
        in_specs=[hbm] * 6,
        out_specs=(whole(), hbm),
        scratch_shapes=[pltpu.VMEM(value.shape, jnp.float32) for value in (loads, lower, weights, right, inverse)]
        + [
            pltpu.VMEM((count, 2 * shots, inner), jnp.float32),
            pltpu.VMEM((size, 2 * shots), jnp.float32),
            pltpu.VMEM((count, size, size), jnp.bfloat16),
            pltpu.VMEM(rows.shape, rows.dtype),
            pltpu.SemaphoreType.DMA((3, count)),
            pltpu.SemaphoreType.DMA,
            pltpu.SemaphoreType.DMA,
            pltpu.SemaphoreType.DMA,
            pltpu.SemaphoreType.DMA((count,)),
        ],
        compiler_params=pltpu.CompilerParams(vmem_limit_bytes=24 * MIB),
        cost_estimate=pl.CostEstimate(flops=40000000000, bytes_accessed=1 << 20, transcendentals=0),
        name="separator_part",
    )(*[in_hbm(value) for value in (loads, lower, weights, rows, right, inverse)])


def joined_blocks(before, lower, weights, rows, eliminated, chosen):
    count, _, size, inner = weights.shape
    shots = eliminated.shape[1] // 2

    def kernel(lower_hbm, weight_hbm, rows_ref, eliminated_hbm, *refs):
        joined_hbm, plain_hbm, lower_ref, weight_ref, eliminated_ref, joined_ref, plain_ref, arrived, left = refs[-9:]
        group = lax.div(lax.axis_index("slab"), GROUP)
        here = group == chosen[0]
        for other in chosen[1:]:
            here = jnp.logical_or(here, group == other)

        def copies(b):
            sources = (lower_hbm, weight_hbm, eliminated_hbm)
            rooms = (lower_ref, weight_ref, eliminated_ref)
            slot = lax.rem(b, 2)
            return [
                pltpu.make_async_copy(source.at[b], room.at[slot], arrived.at[i, slot])
                for i, (source, room) in enumerate(zip(sources, rooms))
            ]

        def leaving(b):
            slot = lax.rem(b, 2)
            return [
                pltpu.make_async_copy(joined_ref.at[slot], joined_hbm.at[b], left.at[0, slot]),
                pltpu.make_async_copy(plain_ref.at[slot], plain_hbm.at[b], left.at[1, slot]),
            ]

        @pl.when(here)
        def _():
            for copy in copies(0):
                copy.start()

            @pl.loop(0, count)
            def _(b):
                slot = lax.rem(b, 2)

                @pl.when(b + 1 < count)
                def _():
                    for copy in copies(b + 1):
                        copy.start()

                @pl.when(b >= 2)
                def _():
                    for copy in leaving(b - 2):
                        copy.wait()

                for copy in copies(b):
                    copy.wait()
                joined = column_product(weight_ref.at[slot], side_by_side(lower_ref.at[slot]))
                joined = spread_product(spread_of(rows_ref[pl.ds(b, 1)]), joined)
                for half in range(2):
                    high, low = split(joined[:, half * inner : (half + 1) * inner])
                    joined_ref[slot, half, 0] = high
                    joined_ref[slot, half, 1] = low
                rows_now = split(eliminated_ref[slot])
                real = near_dot(rows_now, split(lower_ref[slot, 0]))
                imag = near_dot(rows_now, split(lower_ref[slot, 1]))
                plain_ref[slot, :shots] = real[:shots] - imag[shots:]
                plain_ref[slot, shots:] = real[shots:] + imag[:shots]
                for copy in leaving(b):
                    copy.start()

            for b in range(max(0, count - 2), count):
                for copy in leaving(b):
                    copy.wait()

    hbm = pl.BlockSpec(memory_space=pltpu.HBM)
    operands = [in_hbm(lower), in_hbm(weights), rows, in_hbm(eliminated)]
    specs = [hbm, hbm, whole(), hbm]
    aliases = {}
    if before is not None:
        aliases = {4: 0, 5: 1}
        operands += [in_hbm(value) for value in before]
        specs += [hbm] * 2
    return pl.pallas_call(
        kernel,
        out_shape=(
            pltpu.HBM((count, 2, 2, size, inner), jnp.bfloat16),
            pltpu.HBM((count, 2 * shots, inner), jnp.float32),
        ),
        in_specs=specs,
        out_specs=(hbm, hbm),
        scratch_shapes=[
            pltpu.VMEM((2,) + lower.shape[1:], jnp.float32),
            pltpu.VMEM((2,) + weights.shape[1:], jnp.float32),
            pltpu.VMEM((2,) + eliminated.shape[1:], jnp.float32),
            pltpu.VMEM((2, 2, 2, size, inner), jnp.bfloat16),
            pltpu.VMEM((2, 2 * shots, inner), jnp.float32),
            pltpu.SemaphoreType.DMA((3, 2)),
            pltpu.SemaphoreType.DMA((2, 2)),
        ],
        input_output_aliases=aliases,
        compiler_params=pltpu.CompilerParams(vmem_limit_bytes=12 * MIB),
        cost_estimate=LIGHT,
        name="joined_blocks",
    )(*operands)


def finish(arrived, joined, plain):
    count, _, _, size, inner = joined.shape
    pieces, height, _ = arrived.shape
    subs = pieces // GROUP
    width = height // 2
    shots = pieces * width

    def kernel(arrived_ref, joined_hbm, plain_hbm, interior_out, solution_out, joined_ref, plain_ref, solved, landed):
        block = pl.program_id(0)

        def copies(b):
            return [
                pltpu.make_async_copy(joined_hbm.at[b], joined_ref.at[b], landed.at[0, b]),
                pltpu.make_async_copy(plain_hbm.at[b], plain_ref.at[b], landed.at[1, b]),
            ]

        @pl.when(block == 0)
        def _():
            for b in range(count):
                for copy in copies(b):
                    copy.start()
            for half in range(2):
                for sub in range(subs):
                    for member in range(GROUP):
                        start = half * shots + (sub * GROUP + member) * width
                        solved[start : start + width] = arrived_ref[
                            member * subs + sub, half * width : (half + 1) * width
                        ]
                solution_out[half] = solved[half * shots : (half + 1) * shots].T

        for copy in copies(block):
            copy.wait()
        rows_now = split(solved[...])
        real = near_dot(rows_now, (joined_ref[block, 0, 0], joined_ref[block, 0, 1]))
        imag = near_dot(rows_now, (joined_ref[block, 1, 0], joined_ref[block, 1, 1]))
        interior_out[0, 0] = (plain_ref[block, :shots] - (real[:shots] - imag[shots:])).T
        interior_out[0, 1] = (plain_ref[block, shots:] - (real[shots:] + imag[:shots])).T

    hbm = pl.BlockSpec(memory_space=pltpu.HBM)
    return pl.pallas_call(
        kernel,
        grid=(count,),
        out_shape=(
            jax.ShapeDtypeStruct((count, 2, inner, shots), jnp.float32),
            jax.ShapeDtypeStruct((2, size, shots), jnp.float32),
        ),
        in_specs=[whole(), hbm, hbm],
        out_specs=(
            pl.BlockSpec((1, 2, inner, shots), lambda b: (b, 0, 0, 0)),
            pl.BlockSpec((2, size, shots), lambda b: (0, 0, 0)),
        ),
        scratch_shapes=[
            pltpu.VMEM(joined.shape, joined.dtype),
            pltpu.VMEM(plain.shape, plain.dtype),
            pltpu.VMEM((2 * shots, size), jnp.float32),
            pltpu.SemaphoreType.DMA((2, count)),
        ],
        compiler_params=pltpu.CompilerParams(vmem_limit_bytes=16 * MIB),
        name="finish",
    )(arrived, in_hbm(joined), in_hbm(plain))


def turn(state, answer, incoming, blocks, group, forward, backward):
    shape = state.shape[1:]
    subs = answer.shape[1]

    def kernel(*refs):
        state_in, _, block_ref = refs[:3]
        incoming_ref = None if incoming is None else refs[3]
        state_out, answer_out, _, carry = refs[-4:]
        position = lax.axis_index("slab")
        member = lax.rem(position, GROUP)

        @pl.when(lax.div(position, GROUP) == group)
        def _():
            value = None if incoming is None else incoming_ref[...]
            if forward:
                for i in range(GROUP):
                    slot = member ^ i
                    local = state_in[slot]
                    if value is None:
                        value = local
                    else:
                        value = local - row_product(value, block_ref, slot, dot_flipped)
                    state_out[slot] = value
                carry[...] = value
            if backward:
                value = None if forward else value
                for i in reversed(range(GROUP)):
                    slot = member ^ i
                    trace = state_out[slot] if forward else state_in[slot]
                    value = trace if value is None else trace - value
                    for sub in range(subs):
                        answer_out[i, sub] = value
                    if i or group:
                        value = row_product(value, block_ref, slot, dot)
                carry[...] = value

    operands = (state, answer, blocks) + (() if incoming is None else (incoming,))
    return pl.pallas_call(
        kernel,
        out_shape=(
            jax.ShapeDtypeStruct(state.shape, jnp.float32),
            jax.ShapeDtypeStruct(answer.shape, jnp.float32),
            pltpu.VMEM(blocks.shape, blocks.dtype),
            jax.ShapeDtypeStruct(shape, jnp.float32),
        ),
        in_specs=[whole()] * len(operands),
        out_specs=(whole(),) * 4,
        input_output_aliases={0: 0, 1: 1, 2: 2},
        compiler_params=pltpu.CompilerParams(vmem_limit_bytes=16 * MIB),
        name="sweep_turn",
    )(*operands)


def body(
    rhs_interior,
    rhs_separator,
    inverse_blocks,
    coupling,
    separator_rows,
    separator_inverse,
    transfer,
):
    slabs, subs = lax.axis_size("slab"), lax.axis_size("sub")
    member = lax.rem(lax.axis_index("slab"), GROUP)
    turns = slabs // GROUP
    loads, lower, weights, rows = rhs_interior[0], inverse_blocks[0], coupling[0], separator_rows[0]
    groups = [
        [(g * GROUP + m) * subs + u for m in range(GROUP) for u in range(subs)] for g in range(turns)
    ]

    def exchange(value):
        return lax.all_to_all(value, ("slab", "sub"), 0, 0, axis_index_groups=groups, tiled=True)

    own = transfer[0].reshape(-1, transfer.shape[-1])
    crossed, near = crossed_blocks(own, swap(own, 1))
    near, rows = lax.optimization_barrier((near, rows))
    terms, eliminated = separator_part(
        loads, lower, weights, rows, rhs_separator[0], separator_inverse[0]
    )
    crossed[:RELAYED], terms = lax.optimization_barrier((crossed[:RELAYED], terms))
    pieces = [piece for c in range(RELAYED) for piece in relayed_pieces(c, crossed[c])]
    pieces += [(c, 0, crossed[c]) for c in range(RELAYED, RELAYED + DIRECT)]
    terms = exchange(terms)
    early = [swap(piece, 1) if k == 0 and c < RELAYED else None for c, k, piece in pieces]
    settled, terms = lax.optimization_barrier(([piece for _, _, piece in pieces], terms))
    pieces = [(c, k, piece) for (c, k, _), piece in zip(pieces, settled)]
    far = [swap(piece, 1) if sent is None else sent for piece, sent in zip(settled, early)]
    blocks, state = split_blocks(own, near, pieces, far, terms)

    def hop(value, source, steps):
        return move(
            value,
            lambda slab, sub: (slab + GROUP * steps, sub) if slab // GROUP == source else None,
        )

    incoming = joined = None
    answer = jnp.zeros((GROUP, subs) + state.shape[1:], jnp.float32)
    for group in range(turns):
        last = group == turns - 1
        state, answer, blocks, carry = turn(state, answer, incoming, blocks, group, True, last)
        if not last:
            incoming = hop(carry, group, 1)
    for group in reversed(range(turns - 1)):
        incoming = hop(carry, group + 1, -1)
        if group >= turns - 3:
            carry, eliminated = lax.optimization_barrier((carry, eliminated))
            late = group == turns - 3
            chosen = [turns - 2] if late else [g for g in range(turns) if g != turns - 2]
            joined = joined_blocks(joined, lower, weights, rows, eliminated, chosen)
            state, joined = lax.optimization_barrier((state, joined))
        state, answer, blocks, carry = turn(state, answer, incoming, blocks, group, False, True)

    arrived = exchange(answer.reshape((GROUP * subs,) + answer.shape[2:]))
    interior, solved = finish(arrived, *joined)
    return (interior[None], solved[None])


def solution(mesh):
    in_specs = (
        P("slab", "sub", None, None, None),
        P("slab", None, None, None),
        P("slab", "sub", None, None, None),
        P("slab", "sub", None, None, None),
        P("slab", "sub", None),
        P("slab", None, None, None),
        P("slab", None, None, None),
    )
    out_specs = (P("slab", "sub", None, None, None), P("slab", None, None, None))
    return jax.shard_map(body, mesh=mesh, in_specs=in_specs, out_specs=out_specs, check_vma=False)
```

```python
import jax
import jax.numpy as jnp
from jax import lax
from jax.experimental import pallas as pl
from jax.experimental.pallas import tpu as pltpu
from jax.sharding import PartitionSpec as P

GROUP = 4
RELAYED = 1
DIRECT = 1
AHEAD = 2
MIB = 1 << 20
LIGHT = pl.CostEstimate(flops=1, bytes_accessed=1, transcendentals=0)


def move(value, target):
    slabs, subs = lax.axis_size("slab"), lax.axis_size("sub")
    pairs = []
    for slab in range(slabs):
        for sub in range(subs):
            goal = target(slab, sub)
            if goal is not None:
                pairs.append((slab * subs + sub, goal[0] * subs + goal[1]))
    return lax.ppermute(value, ("slab", "sub"), pairs)


def swap(value, mask):
    return move(value, lambda slab, sub: (slab ^ mask, sub))


def shift_sub(value, steps):
    subs = lax.axis_size("sub")
    return move(value, lambda slab, sub: (slab, (sub + steps) % subs))


def pick(array, index):
    return lax.dynamic_index_in_dim(array, index, 0, keepdims=False)


def split(value):
    high = value.astype(jnp.bfloat16)
    return high, (value - high.astype(jnp.float32)).astype(jnp.bfloat16)


def dot(left, right):
    return jnp.dot(left, right, preferred_element_type=jnp.float32)


def dot_flipped(left, right):
    return lax.dot_general(left, right, (((1,), (1,)), ((), ())), preferred_element_type=jnp.float32)


def row_product(rows, matrix, slot, product):
    half = rows.shape[0] // 2
    size = rows.shape[1]
    high, low = split(rows)
    both = jnp.concatenate([high, low], axis=0)

    def against(start):
        wide = product(both, matrix[slot, 0, start : start + size])
        return wide[: 2 * half] + wide[2 * half :] + product(high, matrix[slot, 1, start : start + size])

    real, imag = against(0), against(size)
    return real + jnp.concatenate([-imag[half:], imag[:half]], axis=0)


def whole():
    return pl.BlockSpec(memory_space=pltpu.VMEM)


def plan(size, subs):
    step = 5 * size // 4 // RELAYED // subs
    direct = (2 * size - RELAYED * step * subs) // DIRECT
    return step, direct


def crossed_blocks(own, near):
    subs = lax.axis_size("sub")
    part = lax.axis_index("sub")
    step, direct = plan(own.shape[1], subs)
    shares = [
        lax.dynamic_slice_in_dim(own, (c * subs + part) * step, step, 0) for c in range(RELAYED)
    ]
    crossed = [swap(share, 2) for share in shares]
    start = RELAYED * subs * step
    for c in range(DIRECT):
        share, near = lax.optimization_barrier((own[start + c * direct : start + (c + 1) * direct], near))
        crossed.append(swap(share, 2))
    return crossed, near


def relayed_pieces(c, chunk):
    subs = lax.axis_size("sub")
    now = [chunk] + [shift_sub(chunk, k) for k in range(1, subs)]
    return [(c, k, piece) for k, piece in enumerate(now)]


def in_hbm(value):
    return pltpu.with_memory_space_constraint(value, pltpu.HBM)


def split_blocks(own, near, pieces, far, terms):
    subs = lax.axis_size("sub")
    size = own.shape[1]
    step, direct = plan(size, subs)
    values = [own, near] + [piece for _, _, piece in pieces] + list(far)
    count = len(pieces)

    def kernel(*refs):
        sources, (terms_ref, out, state) = refs[: len(values)], refs[len(values) : len(values) + 3]
        here = lax.axis_index("sub")
        member = lax.rem(lax.axis_index("slab"), GROUP)
        for slot in range(GROUP):
            value = terms_ref[(member ^ slot) * subs]
            for sub in range(1, subs):
                value = value + terms_ref[(member ^ slot) * subs + sub]
            state[slot] = value
        for i, source in enumerate(sources):
            if i < 2:
                out[i, 0], out[i, 1] = split(source[...])
                continue
            slot, (c, k, _) = 2 + (i - 2) // count, pieces[(i - 2) % count]
            if c < RELAYED:
                start = pl.multiple_of((c * subs + lax.rem(here - k + subs, subs)) * step, step)
                rows = pl.ds(start, step)
            else:
                start = RELAYED * subs * step + (c - RELAYED) * direct
                rows = pl.ds(start, direct)
            out[slot, 0, rows], out[slot, 1, rows] = split(source[...])

    return pl.pallas_call(
        kernel,
        out_shape=(
            pltpu.VMEM((GROUP, 2, 2 * size, size), jnp.bfloat16),
            jax.ShapeDtypeStruct((GROUP,) + terms.shape[1:], jnp.float32),
        ),
        in_specs=[whole()] * (len(values) + 1),
        out_specs=(whole(), whole()),
        compiler_params=pltpu.CompilerParams(vmem_limit_bytes=16 * MIB),
        name="split_blocks",
    )(*values, terms)


def near_dot(left, right):
    return dot(left[0], right[0]) + (dot(left[0], right[1]) + dot(left[1], right[0]))


def column_product(matrix, columns):
    half = columns.shape[1] // 2
    columns = split(columns)
    real = near_dot(split(matrix[0]), columns)
    imag = near_dot(split(matrix[1]), columns)
    return jnp.concatenate(
        [real[:, :half] - imag[:, half:], real[:, half:] + imag[:, :half]], axis=1
    )


def side_by_side(pair):
    return jnp.concatenate([pair[0], pair[1]], axis=1)


def spread_of(rows):
    count = rows.shape[1]
    place = lax.broadcasted_iota(jnp.int32, (count, count), 0)
    return jnp.where(rows == place, 1.0, 0.0).astype(jnp.bfloat16)


def spread_product(spread, columns):
    high, low = split(columns)
    return dot(spread, high) + dot(spread, low)


def separator_part(loads, lower, weights, rows, right, inverse):
    count, _, inner, shots = loads.shape
    size = right.shape[1]
    subs = lax.axis_size("sub")
    width = shots // (subs * GROUP)

    def kernel(load_hbm, lower_hbm, weight_hbm, rows_hbm, right_hbm, inverse_hbm, out, eliminated_hbm, *scratch):
        load_ref, lower_ref, weight_ref, right_ref, inverse_ref = scratch[:5]
        eliminated_ref, total, spread, rows_ref, arrived, right_arrived, inverse_arrived, rows_arrived, left = scratch[5:]

        def copies(b):
            sources = (load_hbm, lower_hbm, weight_hbm)
            rooms = (load_ref, lower_ref, weight_ref)
            return [
                pltpu.make_async_copy(source.at[b], room.at[b], arrived.at[i, b])
                for i, (source, room) in enumerate(zip(sources, rooms))
            ]

        def leaving(b):
            return pltpu.make_async_copy(eliminated_ref.at[b], eliminated_hbm.at[b], left.at[b])

        right_copy = pltpu.make_async_copy(right_hbm, right_ref, right_arrived)
        inverse_copy = pltpu.make_async_copy(inverse_hbm, inverse_ref, inverse_arrived)
        rows_copy = pltpu.make_async_copy(rows_hbm, rows_ref, rows_arrived)
        rows_copy.start()
        for b in range(min(AHEAD, count)):
            for copy in copies(b):
                copy.start()
        rows_copy.wait()
        for b in range(count):
            spread[b] = spread_of(rows_ref[b : b + 1])
        for b in range(count):
            for copy in copies(b):
                copy.wait()
            if b + AHEAD < count:
                for copy in copies(b + AHEAD):
                    copy.start()
            elif b + AHEAD == count:
                right_copy.start()
                inverse_copy.start()
            eliminated = column_product(lower_ref.at[b], side_by_side(load_ref.at[b]))
            eliminated_ref[b] = eliminated.T
            leaving(b).start()
            coupled = column_product(weight_ref.at[b], eliminated)
            load = spread_product(spread[b], coupled)
            total[...] = total[...] + load if b else load

        right_copy.wait()
        inverse_copy.wait()
        kept = jnp.where(lax.axis_index("sub") == 0, side_by_side(right_ref), 0.0)
        local = column_product(inverse_ref, kept - total[...])
        for half in range(2):
            shot_rows = local[:, half * shots : (half + 1) * shots].T
            for sub in range(subs):
                for member in range(GROUP):
                    start = (sub * GROUP + member) * width
                    out[member * subs + sub, half * width : (half + 1) * width] = shot_rows[
                        start : start + width
                    ]
        for b in range(count):
            leaving(b).wait()

    hbm = pl.BlockSpec(memory_space=pltpu.HBM)
    return pl.pallas_call(
        kernel,
        out_shape=(
            jax.ShapeDtypeStruct((GROUP * subs, 2 * width, size), jnp.float32),
            pltpu.HBM((count, 2 * shots, inner), jnp.float32),
        ),
        in_specs=[hbm] * 6,
        out_specs=(whole(), hbm),
        scratch_shapes=[pltpu.VMEM(value.shape, jnp.float32) for value in (loads, lower, weights, right, inverse)]
        + [
            pltpu.VMEM((count, 2 * shots, inner), jnp.float32),
            pltpu.VMEM((size, 2 * shots), jnp.float32),
            pltpu.VMEM((count, size, size), jnp.bfloat16),
            pltpu.VMEM(rows.shape, rows.dtype),
            pltpu.SemaphoreType.DMA((3, count)),
            pltpu.SemaphoreType.DMA,
            pltpu.SemaphoreType.DMA,
            pltpu.SemaphoreType.DMA,
            pltpu.SemaphoreType.DMA((count,)),
        ],
        compiler_params=pltpu.CompilerParams(vmem_limit_bytes=24 * MIB),
        cost_estimate=pl.CostEstimate(flops=40000000000, bytes_accessed=1 << 20, transcendentals=0),
        name="separator_part",
    )(*[in_hbm(value) for value in (loads, lower, weights, rows, right, inverse)])


def joined_blocks(before, lower, weights, rows, eliminated, turns):
    count, _, size, inner = weights.shape
    shots = eliminated.shape[1] // 2

    def kernel(lower_hbm, weight_hbm, rows_ref, eliminated_hbm, *refs):
        joined_hbm, plain_hbm, lower_ref, weight_ref, eliminated_ref, joined_ref, plain_ref, arrived, left = refs[-9:]
        halves = lax.div(lax.axis_index("slab"), GROUP) == turns - 2
        first = 0 if before is None else count // 2
        last = jnp.where(halves == (before is None), count // 2, count)

        def copies(b):
            sources = (lower_hbm, weight_hbm, eliminated_hbm)
            rooms = (lower_ref, weight_ref, eliminated_ref)
            slot = lax.rem(b, 2)
            return [
                pltpu.make_async_copy(source.at[b], room.at[slot], arrived.at[i, slot])
                for i, (source, room) in enumerate(zip(sources, rooms))
            ]

        def leaving(b):
            slot = lax.rem(b, 2)
            return [
                pltpu.make_async_copy(joined_ref.at[slot], joined_hbm.at[b], left.at[0, slot]),
                pltpu.make_async_copy(plain_ref.at[slot], plain_hbm.at[b], left.at[1, slot]),
            ]

        @pl.when(last > first)
        def _():
            for copy in copies(first):
                copy.start()

            @pl.loop(first, last)
            def _(b):
                slot = lax.rem(b, 2)

                @pl.when(b + 1 < last)
                def _():
                    for copy in copies(b + 1):
                        copy.start()

                @pl.when(b >= first + 2)
                def _():
                    for copy in leaving(b - 2):
                        copy.wait()

                for copy in copies(b):
                    copy.wait()
                joined = column_product(weight_ref.at[slot], side_by_side(lower_ref.at[slot]))
                joined = spread_product(spread_of(rows_ref[pl.ds(b, 1)]), joined)
                for half in range(2):
                    high, low = split(joined[:, half * inner : (half + 1) * inner])
                    joined_ref[slot, half, 0] = high
                    joined_ref[slot, half, 1] = low
                rows_now = split(eliminated_ref[slot])
                real = near_dot(rows_now, split(lower_ref[slot, 0]))
                imag = near_dot(rows_now, split(lower_ref[slot, 1]))
                plain_ref[slot, :shots] = real[:shots] - imag[shots:]
                plain_ref[slot, shots:] = real[shots:] + imag[:shots]
                for copy in leaving(b):
                    copy.start()

            @pl.loop(jnp.maximum(first, last - 2), last)
            def _(b):
                for copy in leaving(b):
                    copy.wait()

    hbm = pl.BlockSpec(memory_space=pltpu.HBM)
    operands = [in_hbm(lower), in_hbm(weights), rows, in_hbm(eliminated)]
    specs = [hbm, hbm, whole(), hbm]
    aliases = {}
    if before is not None:
        aliases = {4: 0, 5: 1}
        operands += [in_hbm(value) for value in before]
        specs += [hbm] * 2
    return pl.pallas_call(
        kernel,
        out_shape=(
            pltpu.HBM((count, 2, 2, size, inner), jnp.bfloat16),
            pltpu.HBM((count, 2 * shots, inner), jnp.float32),
        ),
        in_specs=specs,
        out_specs=(hbm, hbm),
        scratch_shapes=[
            pltpu.VMEM((2,) + lower.shape[1:], jnp.float32),
            pltpu.VMEM((2,) + weights.shape[1:], jnp.float32),
            pltpu.VMEM((2,) + eliminated.shape[1:], jnp.float32),
            pltpu.VMEM((2, 2, 2, size, inner), jnp.bfloat16),
            pltpu.VMEM((2, 2 * shots, inner), jnp.float32),
            pltpu.SemaphoreType.DMA((3, 2)),
            pltpu.SemaphoreType.DMA((2, 2)),
        ],
        input_output_aliases=aliases,
        compiler_params=pltpu.CompilerParams(vmem_limit_bytes=12 * MIB),
        cost_estimate=LIGHT,
        name="joined_blocks",
    )(*operands)


def finish(arrived, joined, plain):
    count, _, _, size, inner = joined.shape
    pieces, height, _ = arrived.shape
    subs = pieces // GROUP
    width = height // 2
    shots = pieces * width

    def kernel(arrived_ref, joined_ref, plain_ref, interior_out, solution_out, solved):
        block = pl.program_id(0)

        @pl.when(block == 0)
        def _():
            for half in range(2):
                for sub in range(subs):
                    for member in range(GROUP):
                        start = half * shots + (sub * GROUP + member) * width
                        solved[start : start + width] = arrived_ref[
                            member * subs + sub, half * width : (half + 1) * width
                        ]
                solution_out[half] = solved[half * shots : (half + 1) * shots].T

        rows_now = split(solved[...])
        real = near_dot(rows_now, (joined_ref[block, 0, 0], joined_ref[block, 0, 1]))
        imag = near_dot(rows_now, (joined_ref[block, 1, 0], joined_ref[block, 1, 1]))
        interior_out[0, 0] = (plain_ref[block, :shots] - (real[:shots] - imag[shots:])).T
        interior_out[0, 1] = (plain_ref[block, shots:] - (real[shots:] + imag[:shots])).T

    return pl.pallas_call(
        kernel,
        grid=(count,),
        out_shape=(
            jax.ShapeDtypeStruct((count, 2, inner, shots), jnp.float32),
            jax.ShapeDtypeStruct((2, size, shots), jnp.float32),
        ),
        in_specs=[whole()] * 3,
        out_specs=(
            pl.BlockSpec((1, 2, inner, shots), lambda b: (b, 0, 0, 0)),
            pl.BlockSpec((2, size, shots), lambda b: (0, 0, 0)),
        ),
        scratch_shapes=[
            pltpu.VMEM((2 * shots, size), jnp.float32),
        ],
        compiler_params=pltpu.CompilerParams(vmem_limit_bytes=16 * MIB),
        name="finish",
    )(arrived, joined, plain)


def flip_blocks(blocks):
    size = blocks.shape[-1]

    def kernel(blocks_ref, out):
        @pl.when(lax.axis_index("slab") >= GROUP)
        def _():
            @pl.loop(0, 4 * GROUP)
            def _(i):
                slot, part, half = lax.div(i, 4), lax.rem(lax.div(i, 2), 2), lax.rem(i, 2)
                rows = pl.ds(pl.multiple_of(half * size, size), size)
                out[slot, part, rows] = blocks_ref[slot, part, rows].T

    return pl.pallas_call(
        kernel,
        out_shape=pltpu.VMEM(blocks.shape, blocks.dtype),
        in_specs=[whole()],
        out_specs=whole(),
        compiler_params=pltpu.CompilerParams(vmem_limit_bytes=12 * MIB),
        cost_estimate=LIGHT,
        name="flip_blocks",
    )(blocks)


def turn(state, answer, incoming, blocks, flipped, group, forward, backward):
    shape = state.shape[1:]
    subs = answer.shape[1]

    def kernel(*refs):
        state_in, _, block_ref = refs[:3]
        incoming_ref = None if incoming is None else refs[3]
        flipped_ref = None if flipped is None else refs[4]
        state_out, answer_out, _, carry = refs[-4:]
        position = lax.axis_index("slab")
        member = lax.rem(position, GROUP)

        @pl.when(lax.div(position, GROUP) == group)
        def _():
            value = None if incoming is None else incoming_ref[...]
            if forward:
                for i in range(GROUP):
                    slot = member ^ i
                    local = state_in[slot]
                    if value is None:
                        value = local
                    elif flipped is None:
                        value = local - row_product(value, block_ref, slot, dot_flipped)
                    else:
                        value = local - row_product(value, flipped_ref, slot, dot)
                    state_out[slot] = value
                carry[...] = value
            if backward:
                value = None if forward else value
                for i in reversed(range(GROUP)):
                    slot = member ^ i
                    trace = state_out[slot] if forward else state_in[slot]
                    value = trace if value is None else trace - value
                    for sub in range(subs):
                        answer_out[i, sub] = value
                    if i or group:
                        value = row_product(value, block_ref, slot, dot)
                carry[...] = value

    operands = (state, answer, blocks) + tuple(x for x in (incoming, flipped) if x is not None)
    return pl.pallas_call(
        kernel,
        out_shape=(
            jax.ShapeDtypeStruct(state.shape, jnp.float32),
            jax.ShapeDtypeStruct(answer.shape, jnp.float32),
            pltpu.VMEM(blocks.shape, blocks.dtype),
            jax.ShapeDtypeStruct(shape, jnp.float32),
        ),
        in_specs=[whole()] * len(operands),
        out_specs=(whole(),) * 4,
        input_output_aliases={0: 0, 1: 1, 2: 2},
        compiler_params=pltpu.CompilerParams(vmem_limit_bytes=16 * MIB),
        name="sweep_turn",
    )(*operands)


def body(
    rhs_interior,
    rhs_separator,
    inverse_blocks,
    coupling,
    separator_rows,
    separator_inverse,
    transfer,
):
    slabs, subs = lax.axis_size("slab"), lax.axis_size("sub")
    member = lax.rem(lax.axis_index("slab"), GROUP)
    turns = slabs // GROUP
    loads, lower, weights, rows = rhs_interior[0], inverse_blocks[0], coupling[0], separator_rows[0]
    groups = [
        [(g * GROUP + m) * subs + u for m in range(GROUP) for u in range(subs)] for g in range(turns)
    ]

    def exchange(value):
        return lax.all_to_all(value, ("slab", "sub"), 0, 0, axis_index_groups=groups, tiled=True)

    own = transfer[0].reshape(-1, transfer.shape[-1])
    crossed, near = crossed_blocks(own, swap(own, 1))
    near, rows = lax.optimization_barrier((near, rows))
    terms, eliminated = separator_part(
        loads, lower, weights, rows, rhs_separator[0], separator_inverse[0]
    )
    crossed[:RELAYED], terms = lax.optimization_barrier((crossed[:RELAYED], terms))
    pieces = [piece for c in range(RELAYED) for piece in relayed_pieces(c, crossed[c])]
    pieces += [(c, 0, crossed[c]) for c in range(RELAYED, RELAYED + DIRECT)]
    terms = exchange(terms)
    early = [swap(piece, 1) if k == 0 and c < RELAYED else None for c, k, piece in pieces]
    settled, terms = lax.optimization_barrier(([piece for _, _, piece in pieces], terms))
    pieces = [(c, k, piece) for (c, k, _), piece in zip(pieces, settled)]
    far = [swap(piece, 1) if sent is None else sent for piece, sent in zip(settled, early)]
    blocks, state = split_blocks(own, near, pieces, far, terms)

    def hop(value, source, steps):
        return move(
            value,
            lambda slab, sub: (slab + GROUP * steps, sub) if slab // GROUP == source else None,
        )

    incoming = joined = flipped = None
    answer = jnp.zeros((GROUP, subs) + state.shape[1:], jnp.float32)
    for group in range(turns):
        last = group == turns - 1
        state, answer, blocks, carry = turn(
            state, answer, incoming, blocks, flipped, group, True, last
        )
        if not last:
            incoming = hop(carry, group, 1)
        if not group:
            state, blocks = lax.optimization_barrier((state, blocks))
            flipped = flip_blocks(blocks)
    for group in reversed(range(turns - 1)):
        incoming = hop(carry, group + 1, -1)
        if group >= turns - 3:
            carry, eliminated = lax.optimization_barrier((carry, eliminated))
            joined = joined_blocks(joined, lower, weights, rows, eliminated, turns)
            state, joined = lax.optimization_barrier((state, joined))
        state, answer, blocks, carry = turn(
            state, answer, incoming, blocks, None, group, False, True
        )

    arrived = exchange(answer.reshape((GROUP * subs,) + answer.shape[2:]))
    interior, solved = finish(arrived, *joined)
    return (interior[None], solved[None])


def solution(mesh):
    in_specs = (
        P("slab", "sub", None, None, None),
        P("slab", None, None, None),
        P("slab", "sub", None, None, None),
        P("slab", "sub", None, None, None),
        P("slab", "sub", None),
        P("slab", None, None, None),
        P("slab", None, None, None),
    )
    out_specs = (P("slab", "sub", None, None, None), P("slab", None, None, None))
    return jax.shard_map(body, mesh=mesh, in_specs=in_specs, out_specs=out_specs, check_vma=False)
```

```python
import jax
import jax.numpy as jnp
from jax import lax
from jax.experimental import pallas as pl
from jax.experimental.pallas import tpu as pltpu
from jax.sharding import PartitionSpec as P

GROUP = 4
RELAYED = 1
DIRECT = 1
AHEAD = 2
MIB = 1 << 20
LIGHT = pl.CostEstimate(flops=1, bytes_accessed=1, transcendentals=0)


def move(value, target):
    slabs, subs = lax.axis_size("slab"), lax.axis_size("sub")
    pairs = []
    for slab in range(slabs):
        for sub in range(subs):
            goal = target(slab, sub)
            if goal is not None:
                pairs.append((slab * subs + sub, goal[0] * subs + goal[1]))
    return lax.ppermute(value, ("slab", "sub"), pairs)


def swap(value, mask):
    return move(value, lambda slab, sub: (slab ^ mask, sub))


def shift_sub(value, steps):
    subs = lax.axis_size("sub")
    return move(value, lambda slab, sub: (slab, (sub + steps) % subs))


def pick(array, index):
    return lax.dynamic_index_in_dim(array, index, 0, keepdims=False)


def split(value):
    high = value.astype(jnp.bfloat16)
    return high, (value - high.astype(jnp.float32)).astype(jnp.bfloat16)


def dot(left, right):
    return jnp.dot(left, right, preferred_element_type=jnp.float32)


def dot_flipped(left, right):
    return lax.dot_general(left, right, (((1,), (1,)), ((), ())), preferred_element_type=jnp.float32)


def row_product(rows, matrix, slot, product):
    half = rows.shape[0] // 2
    size = rows.shape[1]
    high, low = split(rows)
    both = jnp.concatenate([high, low], axis=0)

    def against(start):
        wide = product(both, matrix[slot, 0, start : start + size])
        return wide[: 2 * half] + wide[2 * half :] + product(high, matrix[slot, 1, start : start + size])

    real, imag = against(0), against(size)
    return real + jnp.concatenate([-imag[half:], imag[:half]], axis=0)


def whole():
    return pl.BlockSpec(memory_space=pltpu.VMEM)


def plan(size, subs):
    step = 5 * size // 4 // RELAYED // subs
    direct = (2 * size - RELAYED * step * subs) // DIRECT
    return step, direct


def crossed_blocks(own, near):
    subs = lax.axis_size("sub")
    part = lax.axis_index("sub")
    step, direct = plan(own.shape[1], subs)
    shares = [
        lax.dynamic_slice_in_dim(own, (c * subs + part) * step, step, 0) for c in range(RELAYED)
    ]
    crossed = [swap(share, 2) for share in shares]
    start = RELAYED * subs * step
    for c in range(DIRECT):
        share, near = lax.optimization_barrier((own[start + c * direct : start + (c + 1) * direct], near))
        crossed.append(swap(share, 2))
    return crossed, near


def relayed_pieces(c, chunk):
    subs = lax.axis_size("sub")
    now = [chunk] + [shift_sub(chunk, k) for k in range(1, subs)]
    return [(c, k, piece) for k, piece in enumerate(now)]


def in_hbm(value):
    return pltpu.with_memory_space_constraint(value, pltpu.HBM)


def split_blocks(own, near, pieces, far, terms):
    subs = lax.axis_size("sub")
    size = own.shape[1]
    step, direct = plan(size, subs)
    values = [own, near] + [piece for _, _, piece in pieces] + list(far)
    count = len(pieces)

    def kernel(*refs):
        sources, (terms_ref, out, state) = refs[: len(values)], refs[len(values) : len(values) + 3]
        here = lax.axis_index("sub")
        member = lax.rem(lax.axis_index("slab"), GROUP)
        for slot in range(GROUP):
            value = terms_ref[(member ^ slot) * subs]
            for sub in range(1, subs):
                value = value + terms_ref[(member ^ slot) * subs + sub]
            state[slot] = value
        for i, source in enumerate(sources):
            if i < 2:
                out[i, 0], out[i, 1] = split(source[...])
                continue
            slot, (c, k, _) = 2 + (i - 2) // count, pieces[(i - 2) % count]
            if c < RELAYED:
                start = pl.multiple_of((c * subs + lax.rem(here - k + subs, subs)) * step, step)
                rows = pl.ds(start, step)
            else:
                start = RELAYED * subs * step + (c - RELAYED) * direct
                rows = pl.ds(start, direct)
            out[slot, 0, rows], out[slot, 1, rows] = split(source[...])

    return pl.pallas_call(
        kernel,
        out_shape=(
            pltpu.VMEM((GROUP, 2, 2 * size, size), jnp.bfloat16),
            jax.ShapeDtypeStruct((GROUP,) + terms.shape[1:], jnp.float32),
        ),
        in_specs=[whole()] * (len(values) + 1),
        out_specs=(whole(), whole()),
        compiler_params=pltpu.CompilerParams(vmem_limit_bytes=16 * MIB),
        name="split_blocks",
    )(*values, terms)


def near_dot(left, right):
    return dot(left[0], right[0]) + (dot(left[0], right[1]) + dot(left[1], right[0]))


def column_product(matrix, columns):
    half = columns.shape[1] // 2
    columns = split(columns)
    real = near_dot(split(matrix[0]), columns)
    imag = near_dot(split(matrix[1]), columns)
    return jnp.concatenate(
        [real[:, :half] - imag[:, half:], real[:, half:] + imag[:, :half]], axis=1
    )


def side_by_side(pair):
    return jnp.concatenate([pair[0], pair[1]], axis=1)


def spread_of(rows):
    count = rows.shape[1]
    place = lax.broadcasted_iota(jnp.int32, (count, count), 0)
    return jnp.where(rows == place, 1.0, 0.0).astype(jnp.bfloat16)


def spread_product(spread, columns):
    high, low = split(columns)
    return dot(spread, high) + dot(spread, low)


def separator_part(loads, lower, weights, rows, right, inverse):
    count, _, inner, shots = loads.shape
    size = right.shape[1]
    subs = lax.axis_size("sub")
    width = shots // (subs * GROUP)

    def kernel(load_hbm, lower_hbm, weight_hbm, rows_hbm, right_hbm, inverse_hbm, out, eliminated_hbm, *scratch):
        load_ref, lower_ref, weight_ref, right_ref, inverse_ref = scratch[:5]
        eliminated_ref, total, spread, rows_ref, arrived, right_arrived, inverse_arrived, rows_arrived, left = scratch[5:]

        def copies(b):
            sources = (load_hbm, lower_hbm, weight_hbm)
            rooms = (load_ref, lower_ref, weight_ref)
            return [
                pltpu.make_async_copy(source.at[b], room.at[b], arrived.at[i, b])
                for i, (source, room) in enumerate(zip(sources, rooms))
            ]

        def leaving(b):
            return pltpu.make_async_copy(eliminated_ref.at[b], eliminated_hbm.at[b], left.at[b])

        right_copy = pltpu.make_async_copy(right_hbm, right_ref, right_arrived)
        inverse_copy = pltpu.make_async_copy(inverse_hbm, inverse_ref, inverse_arrived)
        rows_copy = pltpu.make_async_copy(rows_hbm, rows_ref, rows_arrived)
        rows_copy.start()
        for b in range(min(AHEAD, count)):
            for copy in copies(b):
                copy.start()
        rows_copy.wait()
        for b in range(count):
            spread[b] = spread_of(rows_ref[b : b + 1])
        for pair in range(0, count, 2):
            now = range(pair, min(pair + 2, count))
            for b in now:
                for copy in copies(b):
                    copy.wait()
            for b in now:
                if b + 2 < count:
                    for copy in copies(b + 2):
                        copy.start()
            if pair + 2 >= count:
                right_copy.start()
                inverse_copy.start()
            eliminated = [column_product(lower_ref.at[b], side_by_side(load_ref.at[b])) for b in now]
            for b, value in zip(now, eliminated):
                eliminated_ref[b] = value.T
                leaving(b).start()
            coupled = [column_product(weight_ref.at[b], value) for b, value in zip(now, eliminated)]
            load = sum(spread_product(spread[b], value) for b, value in zip(now, coupled))
            total[...] = total[...] + load if pair else load

        right_copy.wait()
        inverse_copy.wait()
        kept = jnp.where(lax.axis_index("sub") == 0, side_by_side(right_ref), 0.0)
        local = column_product(inverse_ref, kept - total[...])
        for half in range(2):
            shot_rows = local[:, half * shots : (half + 1) * shots].T
            for sub in range(subs):
                for member in range(GROUP):
                    start = (sub * GROUP + member) * width
                    out[member * subs + sub, half * width : (half + 1) * width] = shot_rows[
                        start : start + width
                    ]
        for b in range(count):
            leaving(b).wait()

    hbm = pl.BlockSpec(memory_space=pltpu.HBM)
    return pl.pallas_call(
        kernel,
        out_shape=(
            jax.ShapeDtypeStruct((GROUP * subs, 2 * width, size), jnp.float32),
            pltpu.HBM((count, 2 * shots, inner), jnp.float32),
        ),
        in_specs=[hbm] * 6,
        out_specs=(whole(), hbm),
        scratch_shapes=[pltpu.VMEM(value.shape, jnp.float32) for value in (loads, lower, weights, right, inverse)]
        + [
            pltpu.VMEM((count, 2 * shots, inner), jnp.float32),
            pltpu.VMEM((size, 2 * shots), jnp.float32),
            pltpu.VMEM((count, size, size), jnp.bfloat16),
            pltpu.VMEM(rows.shape, rows.dtype),
            pltpu.SemaphoreType.DMA((3, count)),
            pltpu.SemaphoreType.DMA,
            pltpu.SemaphoreType.DMA,
            pltpu.SemaphoreType.DMA,
            pltpu.SemaphoreType.DMA((count,)),
        ],
        compiler_params=pltpu.CompilerParams(vmem_limit_bytes=24 * MIB),
        cost_estimate=pl.CostEstimate(flops=40000000000, bytes_accessed=1 << 20, transcendentals=0),
        name="separator_part",
    )(*[in_hbm(value) for value in (loads, lower, weights, rows, right, inverse)])


def joined_blocks(before, lower, weights, rows, eliminated, turns):
    count, _, size, inner = weights.shape
    shots = eliminated.shape[1] // 2

    def kernel(lower_hbm, weight_hbm, rows_ref, eliminated_hbm, *refs):
        joined_hbm, plain_hbm, lower_ref, weight_ref, eliminated_ref, joined_ref, plain_ref, arrived, left = refs[-9:]
        halves = lax.div(lax.axis_index("slab"), GROUP) == turns - 2
        first = 0 if before is None else count // 2
        last = jnp.where(halves == (before is None), count // 2, count)

        def copies(b):
            sources = (lower_hbm, weight_hbm, eliminated_hbm)
            rooms = (lower_ref, weight_ref, eliminated_ref)
            slot = lax.rem(b, 2)
            return [
                pltpu.make_async_copy(source.at[b], room.at[slot], arrived.at[i, slot])
                for i, (source, room) in enumerate(zip(sources, rooms))
            ]

        def leaving(b):
            slot = lax.rem(b, 2)
            return [
                pltpu.make_async_copy(joined_ref.at[slot], joined_hbm.at[b], left.at[0, slot]),
                pltpu.make_async_copy(plain_ref.at[slot], plain_hbm.at[b], left.at[1, slot]),
            ]

        @pl.when(last > first)
        def _():
            for copy in copies(first):
                copy.start()

            @pl.loop(first, last)
            def _(b):
                slot = lax.rem(b, 2)

                @pl.when(b + 1 < last)
                def _():
                    for copy in copies(b + 1):
                        copy.start()

                @pl.when(b >= first + 2)
                def _():
                    for copy in leaving(b - 2):
                        copy.wait()

                for copy in copies(b):
                    copy.wait()
                joined = column_product(weight_ref.at[slot], side_by_side(lower_ref.at[slot]))
                joined = spread_product(spread_of(rows_ref[pl.ds(b, 1)]), joined)
                for half in range(2):
                    high, low = split(joined[:, half * inner : (half + 1) * inner])
                    joined_ref[slot, half, 0] = high
                    joined_ref[slot, half, 1] = low
                rows_now = split(eliminated_ref[slot])
                real = near_dot(rows_now, split(lower_ref[slot, 0]))
                imag = near_dot(rows_now, split(lower_ref[slot, 1]))
                plain_ref[slot, :shots] = real[:shots] - imag[shots:]
                plain_ref[slot, shots:] = real[shots:] + imag[:shots]
                for copy in leaving(b):
                    copy.start()

            @pl.loop(jnp.maximum(first, last - 2), last)
            def _(b):
                for copy in leaving(b):
                    copy.wait()

    hbm = pl.BlockSpec(memory_space=pltpu.HBM)
    operands = [in_hbm(lower), in_hbm(weights), rows, in_hbm(eliminated)]
    specs = [hbm, hbm, whole(), hbm]
    aliases = {}
    if before is not None:
        aliases = {4: 0, 5: 1}
        operands += [in_hbm(value) for value in before]
        specs += [hbm] * 2
    return pl.pallas_call(
        kernel,
        out_shape=(
            pltpu.HBM((count, 2, 2, size, inner), jnp.bfloat16),
            pltpu.HBM((count, 2 * shots, inner), jnp.float32),
        ),
        in_specs=specs,
        out_specs=(hbm, hbm),
        scratch_shapes=[
            pltpu.VMEM((2,) + lower.shape[1:], jnp.float32),
            pltpu.VMEM((2,) + weights.shape[1:], jnp.float32),
            pltpu.VMEM((2,) + eliminated.shape[1:], jnp.float32),
            pltpu.VMEM((2, 2, 2, size, inner), jnp.bfloat16),
            pltpu.VMEM((2, 2 * shots, inner), jnp.float32),
            pltpu.SemaphoreType.DMA((3, 2)),
            pltpu.SemaphoreType.DMA((2, 2)),
        ],
        input_output_aliases=aliases,
        compiler_params=pltpu.CompilerParams(vmem_limit_bytes=12 * MIB),
        cost_estimate=LIGHT,
        name="joined_blocks",
    )(*operands)


def finish(arrived, joined, plain):
    count, _, _, size, inner = joined.shape
    pieces, height, _ = arrived.shape
    subs = pieces // GROUP
    width = height // 2
    shots = pieces * width

    def kernel(arrived_ref, joined_ref, plain_ref, interior_hbm, solution_hbm, solved, interior, solution, left):
        for half in range(2):
            for sub in range(subs):
                for member in range(GROUP):
                    start = half * shots + (sub * GROUP + member) * width
                    solved[start : start + width] = arrived_ref[
                        member * subs + sub, half * width : (half + 1) * width
                    ]
        rows_now = split(solved[...])
        for half in range(2):
            solution[half] = solved[half * shots : (half + 1) * shots].T
        copies = [pltpu.make_async_copy(solution, solution_hbm, left.at[count])]
        copies[0].start()
        for block in range(count):
            real = near_dot(rows_now, (joined_ref[block, 0, 0], joined_ref[block, 0, 1]))
            imag = near_dot(rows_now, (joined_ref[block, 1, 0], joined_ref[block, 1, 1]))
            interior[block, 0] = (plain_ref[block, :shots] - (real[:shots] - imag[shots:])).T
            interior[block, 1] = (plain_ref[block, shots:] - (real[shots:] + imag[:shots])).T
            copies.append(
                pltpu.make_async_copy(interior.at[block], interior_hbm.at[block], left.at[block])
            )
            copies[-1].start()
        for copy in copies:
            copy.wait()

    hbm = pl.BlockSpec(memory_space=pltpu.HBM)
    return pl.pallas_call(
        kernel,
        out_shape=(
            pltpu.HBM((count, 2, inner, shots), jnp.float32),
            pltpu.HBM((2, size, shots), jnp.float32),
        ),
        in_specs=[whole()] * 3,
        out_specs=(hbm, hbm),
        scratch_shapes=[
            pltpu.VMEM((2 * shots, size), jnp.float32),
            pltpu.VMEM((count, 2, inner, shots), jnp.float32),
            pltpu.VMEM((2, size, shots), jnp.float32),
            pltpu.SemaphoreType.DMA((count + 1,)),
        ],
        compiler_params=pltpu.CompilerParams(vmem_limit_bytes=12 * MIB),
        name="finish",
    )(arrived, joined, plain)


def flip_blocks(blocks):
    size = blocks.shape[-1]

    def kernel(blocks_ref, out):
        @pl.when(lax.axis_index("slab") >= GROUP)
        def _():
            @pl.loop(0, 4 * GROUP)
            def _(i):
                slot, part, half = lax.div(i, 4), lax.rem(lax.div(i, 2), 2), lax.rem(i, 2)
                rows = pl.ds(pl.multiple_of(half * size, size), size)
                out[slot, part, rows] = blocks_ref[slot, part, rows].T

    return pl.pallas_call(
        kernel,
        out_shape=pltpu.VMEM(blocks.shape, blocks.dtype),
        in_specs=[whole()],
        out_specs=whole(),
        compiler_params=pltpu.CompilerParams(vmem_limit_bytes=12 * MIB),
        cost_estimate=LIGHT,
        name="flip_blocks",
    )(blocks)


def turn(state, answer, incoming, blocks, flipped, group, forward, backward):
    shape = state.shape[1:]
    subs = answer.shape[1]

    def kernel(*refs):
        state_in, _, block_ref = refs[:3]
        incoming_ref = None if incoming is None else refs[3]
        flipped_ref = None if flipped is None else refs[4]
        state_out, answer_out, _, carry = refs[-4:]
        position = lax.axis_index("slab")
        member = lax.rem(position, GROUP)

        @pl.when(lax.div(position, GROUP) == group)
        def _():
            value = None if incoming is None else incoming_ref[...]
            if forward:
                for i in range(GROUP):
                    slot = member ^ i
                    local = state_in[slot]
                    if value is None:
                        value = local
                    elif flipped is None:
                        value = local - row_product(value, block_ref, slot, dot_flipped)
                    else:
                        value = local - row_product(value, flipped_ref, slot, dot)
                    state_out[slot] = value
                carry[...] = value
            if backward:
                value = None if forward else value
                for i in reversed(range(GROUP)):
                    slot = member ^ i
                    trace = state_out[slot] if forward else state_in[slot]
                    value = trace if value is None else trace - value
                    for sub in range(subs):
                        answer_out[i, sub] = value
                    if i or group:
                        value = row_product(value, block_ref, slot, dot)
                carry[...] = value

    operands = (state, answer, blocks) + tuple(x for x in (incoming, flipped) if x is not None)
    return pl.pallas_call(
        kernel,
        out_shape=(
            jax.ShapeDtypeStruct(state.shape, jnp.float32),
            jax.ShapeDtypeStruct(answer.shape, jnp.float32),
            pltpu.VMEM(blocks.shape, blocks.dtype),
            jax.ShapeDtypeStruct(shape, jnp.float32),
        ),
        in_specs=[whole()] * len(operands),
        out_specs=(whole(),) * 4,
        input_output_aliases={0: 0, 1: 1, 2: 2},
        compiler_params=pltpu.CompilerParams(vmem_limit_bytes=16 * MIB),
        name="sweep_turn",
    )(*operands)


def body(
    rhs_interior,
    rhs_separator,
    inverse_blocks,
    coupling,
    separator_rows,
    separator_inverse,
    transfer,
):
    slabs, subs = lax.axis_size("slab"), lax.axis_size("sub")
    member = lax.rem(lax.axis_index("slab"), GROUP)
    turns = slabs // GROUP
    loads, lower, weights, rows = rhs_interior[0], inverse_blocks[0], coupling[0], separator_rows[0]
    groups = [
        [(g * GROUP + m) * subs + u for m in range(GROUP) for u in range(subs)] for g in range(turns)
    ]

    def exchange(value):
        return lax.all_to_all(value, ("slab", "sub"), 0, 0, axis_index_groups=groups, tiled=True)

    own = transfer[0].reshape(-1, transfer.shape[-1])
    crossed, near = crossed_blocks(own, swap(own, 1))
    near, rows = lax.optimization_barrier((near, rows))
    terms, eliminated = separator_part(
        loads, lower, weights, rows, rhs_separator[0], separator_inverse[0]
    )
    crossed[:RELAYED], terms = lax.optimization_barrier((crossed[:RELAYED], terms))
    pieces = [piece for c in range(RELAYED) for piece in relayed_pieces(c, crossed[c])]
    pieces += [(c, 0, crossed[c]) for c in range(RELAYED, RELAYED + DIRECT)]
    terms = exchange(terms)
    early = [swap(piece, 1) if k == 0 and c < RELAYED else None for c, k, piece in pieces]
    settled, terms = lax.optimization_barrier(([piece for _, _, piece in pieces], terms))
    pieces = [(c, k, piece) for (c, k, _), piece in zip(pieces, settled)]
    far = [swap(piece, 1) if sent is None else sent for piece, sent in zip(settled, early)]
    blocks, state = split_blocks(own, near, pieces, far, terms)

    def hop(value, source, steps):
        return move(
            value,
            lambda slab, sub: (slab + GROUP * steps, sub) if slab // GROUP == source else None,
        )

    incoming = joined = flipped = None
    answer = jnp.zeros((GROUP, subs) + state.shape[1:], jnp.float32)
    for group in range(turns):
        last = group == turns - 1
        state, answer, blocks, carry = turn(
            state, answer, incoming, blocks, flipped, group, True, last
        )
        if not last:
            incoming = hop(carry, group, 1)
        if not group:
            state, blocks = lax.optimization_barrier((state, blocks))
            flipped = flip_blocks(blocks)
    for group in reversed(range(turns - 1)):
        incoming = hop(carry, group + 1, -1)
        if group >= turns - 3:
            carry, eliminated = lax.optimization_barrier((carry, eliminated))
            joined = joined_blocks(joined, lower, weights, rows, eliminated, turns)
            state, joined = lax.optimization_barrier((state, joined))
        state, answer, blocks, carry = turn(
            state, answer, incoming, blocks, None, group, False, True
        )

    arrived = exchange(answer.reshape((GROUP * subs,) + answer.shape[2:]))
    interior, solved = finish(arrived, *joined)
    return (interior[None], solved[None])


def solution(mesh):
    in_specs = (
        P("slab", "sub", None, None, None),
        P("slab", None, None, None),
        P("slab", "sub", None, None, None),
        P("slab", "sub", None, None, None),
        P("slab", "sub", None),
        P("slab", None, None, None),
        P("slab", None, None, None),
    )
    out_specs = (P("slab", "sub", None, None, None), P("slab", None, None, None))
    return jax.shard_map(body, mesh=mesh, in_specs=in_specs, out_specs=out_specs, check_vma=False)
```

```python
import jax
import jax.numpy as jnp
from jax import lax
from jax.experimental import pallas as pl
from jax.experimental.pallas import tpu as pltpu
from jax.sharding import PartitionSpec as P

GROUP = 4
RELAYED = 1
DIRECT = 1
AHEAD = 2
MIB = 1 << 20
LIGHT = pl.CostEstimate(flops=1, bytes_accessed=1, transcendentals=0)
HEAVY = pl.CostEstimate(flops=10**9, bytes_accessed=1 << 24, transcendentals=0)


def move(value, target):
    slabs, subs = lax.axis_size("slab"), lax.axis_size("sub")
    pairs = []
    for slab in range(slabs):
        for sub in range(subs):
            goal = target(slab, sub)
            if goal is not None:
                pairs.append((slab * subs + sub, goal[0] * subs + goal[1]))
    return lax.ppermute(value, ("slab", "sub"), pairs)


def swap(value, mask):
    return move(value, lambda slab, sub: (slab ^ mask, sub))


def shift_sub(value, steps):
    subs = lax.axis_size("sub")
    return move(value, lambda slab, sub: (slab, (sub + steps) % subs))


def pick(array, index):
    return lax.dynamic_index_in_dim(array, index, 0, keepdims=False)


def split(value):
    high = value.astype(jnp.bfloat16)
    return high, (value - high.astype(jnp.float32)).astype(jnp.bfloat16)


def dot(left, right):
    return jnp.dot(left, right, preferred_element_type=jnp.float32)


def dot_flipped(left, right):
    return lax.dot_general(left, right, (((1,), (1,)), ((), ())), preferred_element_type=jnp.float32)


def row_product(rows, matrix, slot, product):
    half = rows.shape[0] // 2
    size = rows.shape[1]
    high, low = split(rows)
    both = jnp.concatenate([high, low], axis=0)

    def against(start):
        wide = product(both, matrix[slot, 0, start : start + size])
        return wide[: 2 * half] + wide[2 * half :] + product(high, matrix[slot, 1, start : start + size])

    real, imag = against(0), against(size)
    return real + jnp.concatenate([-imag[half:], imag[:half]], axis=0)


def whole():
    return pl.BlockSpec(memory_space=pltpu.VMEM)


def plan(size, subs):
    step = 5 * size // 4 // RELAYED // subs
    direct = (2 * size - RELAYED * step * subs) // DIRECT
    return step, direct


def crossed_blocks(own, near):
    subs = lax.axis_size("sub")
    part = lax.axis_index("sub")
    step, direct = plan(own.shape[1], subs)
    shares = [
        lax.dynamic_slice_in_dim(own, (c * subs + part) * step, step, 0) for c in range(RELAYED)
    ]
    crossed = [swap(share, 2) for share in shares]
    start = RELAYED * subs * step
    for c in range(DIRECT):
        share, near = lax.optimization_barrier((own[start + c * direct : start + (c + 1) * direct], near))
        crossed.append(swap(share, 2))
    return crossed, near


def relayed_pieces(c, chunk):
    subs = lax.axis_size("sub")
    now = [chunk] + [shift_sub(chunk, k) for k in range(1, subs)]
    return [(c, k, piece) for k, piece in enumerate(now)]


def in_hbm(value):
    return pltpu.with_memory_space_constraint(value, pltpu.HBM)


def places(pieces, size):
    subs = lax.axis_size("sub")
    here = lax.axis_index("sub")
    step, direct = plan(size, subs)
    for c, k, _ in pieces:
        if c < RELAYED:
            start = (c * subs + lax.rem(here - k + subs, subs)) * step
            yield pl.ds(pl.multiple_of(start, step), step)
        else:
            yield pl.ds(RELAYED * subs * step + (c - RELAYED) * direct, direct)


def split_blocks(own, near, pieces, terms):
    subs = lax.axis_size("sub")
    size = own.shape[1]
    values = [own, near] + [piece for _, _, piece in pieces]

    def kernel(*refs):
        sources, (terms_ref, out, state) = refs[: len(values)], refs[len(values) :]
        member = lax.rem(lax.axis_index("slab"), GROUP)
        for slot in range(GROUP):
            value = terms_ref[(member ^ slot) * subs]
            for sub in range(1, subs):
                value = value + terms_ref[(member ^ slot) * subs + sub]
            state[slot] = value
        for slot in range(2):
            out[slot, 0], out[slot, 1] = split(sources[slot][...])
        for rows, source in zip(places(pieces, size), sources[2:]):
            out[2, 0, rows], out[2, 1, rows] = split(source[...])

    return pl.pallas_call(
        kernel,
        out_shape=(
            pltpu.VMEM((GROUP, 2, 2 * size, size), jnp.bfloat16),
            jax.ShapeDtypeStruct((GROUP,) + terms.shape[1:], jnp.float32),
        ),
        in_specs=[whole()] * (len(values) + 1),
        out_specs=(whole(), whole()),
        compiler_params=pltpu.CompilerParams(vmem_limit_bytes=16 * MIB),
        cost_estimate=HEAVY,
        name="split_blocks",
    )(*values, terms)


def split_last(blocks, pieces, far):
    def kernel(_, *refs):
        out = refs[-1]
        for rows, source in zip(places(pieces, blocks.shape[-1]), refs[:-1]):
            out[3, 0, rows], out[3, 1, rows] = split(source[...])

    return pl.pallas_call(
        kernel,
        out_shape=pltpu.VMEM(blocks.shape, blocks.dtype),
        in_specs=[whole()] * (1 + len(far)),
        out_specs=whole(),
        input_output_aliases={0: 0},
        compiler_params=pltpu.CompilerParams(vmem_limit_bytes=16 * MIB),
        name="split_last",
    )(blocks, *far)


def near_dot(left, right):
    return dot(left[0], right[0]) + (dot(left[0], right[1]) + dot(left[1], right[0]))


def column_product(matrix, columns):
    half = columns.shape[1] // 2
    columns = split(columns)
    real = near_dot(split(matrix[0]), columns)
    imag = near_dot(split(matrix[1]), columns)
    return jnp.concatenate(
        [real[:, :half] - imag[:, half:], real[:, half:] + imag[:, :half]], axis=1
    )


def side_by_side(pair):
    return jnp.concatenate([pair[0], pair[1]], axis=1)


def spread_of(rows):
    count = rows.shape[1]
    place = lax.broadcasted_iota(jnp.int32, (count, count), 0)
    return jnp.where(rows == place, 1.0, 0.0).astype(jnp.bfloat16)


def spread_product(spread, columns):
    high, low = split(columns)
    return dot(spread, high) + dot(spread, low)


def separator_part(loads, lower, weights, rows, right, inverse):
    count, _, inner, shots = loads.shape
    size = right.shape[1]
    subs = lax.axis_size("sub")
    width = shots // (subs * GROUP)

    def kernel(load_hbm, lower_hbm, weight_hbm, rows_hbm, right_hbm, inverse_hbm, out, eliminated_hbm, *scratch):
        load_ref, lower_ref, weight_ref, right_ref, inverse_ref = scratch[:5]
        eliminated_ref, total, spread, rows_ref, arrived, right_arrived, inverse_arrived, rows_arrived, left = scratch[5:]

        def copies(b):
            sources = (load_hbm, lower_hbm, weight_hbm)
            rooms = (load_ref, lower_ref, weight_ref)
            return [
                pltpu.make_async_copy(source.at[b], room.at[b], arrived.at[i, b])
                for i, (source, room) in enumerate(zip(sources, rooms))
            ]

        def leaving(b):
            return pltpu.make_async_copy(eliminated_ref.at[b], eliminated_hbm.at[b], left.at[b])

        right_copy = pltpu.make_async_copy(right_hbm, right_ref, right_arrived)
        inverse_copy = pltpu.make_async_copy(inverse_hbm, inverse_ref, inverse_arrived)
        rows_copy = pltpu.make_async_copy(rows_hbm, rows_ref, rows_arrived)
        rows_copy.start()
        for b in range(min(AHEAD, count)):
            for copy in copies(b):
                copy.start()
        rows_copy.wait()
        for b in range(count):
            spread[b] = spread_of(rows_ref[b : b + 1])
        for pair in range(0, count, 2):
            now = range(pair, min(pair + 2, count))
            for b in now:
                for copy in copies(b):
                    copy.wait()
            for b in now:
                if b + 2 < count:
                    for copy in copies(b + 2):
                        copy.start()
            if pair + 2 >= count:
                right_copy.start()
                inverse_copy.start()
            eliminated = [column_product(lower_ref.at[b], side_by_side(load_ref.at[b])) for b in now]
            for b, value in zip(now, eliminated):
                eliminated_ref[b] = value.T
                leaving(b).start()
            coupled = [column_product(weight_ref.at[b], value) for b, value in zip(now, eliminated)]
            load = sum(spread_product(spread[b], value) for b, value in zip(now, coupled))
            total[...] = total[...] + load if pair else load

        right_copy.wait()
        inverse_copy.wait()
        kept = jnp.where(lax.axis_index("sub") == 0, side_by_side(right_ref), 0.0)
        local = column_product(inverse_ref, kept - total[...])
        for half in range(2):
            shot_rows = local[:, half * shots : (half + 1) * shots].T
            for sub in range(subs):
                for member in range(GROUP):
                    start = (sub * GROUP + member) * width
                    out[member * subs + sub, half * width : (half + 1) * width] = shot_rows[
                        start : start + width
                    ]
        for b in range(count):
            leaving(b).wait()

    hbm = pl.BlockSpec(memory_space=pltpu.HBM)
    return pl.pallas_call(
        kernel,
        out_shape=(
            jax.ShapeDtypeStruct((GROUP * subs, 2 * width, size), jnp.float32),
            pltpu.HBM((count, 2 * shots, inner), jnp.float32),
        ),
        in_specs=[hbm] * 6,
        out_specs=(whole(), hbm),
        scratch_shapes=[pltpu.VMEM(value.shape, jnp.float32) for value in (loads, lower, weights, right, inverse)]
        + [
            pltpu.VMEM((count, 2 * shots, inner), jnp.float32),
            pltpu.VMEM((size, 2 * shots), jnp.float32),
            pltpu.VMEM((count, size, size), jnp.bfloat16),
            pltpu.VMEM(rows.shape, rows.dtype),
            pltpu.SemaphoreType.DMA((3, count)),
            pltpu.SemaphoreType.DMA,
            pltpu.SemaphoreType.DMA,
            pltpu.SemaphoreType.DMA,
            pltpu.SemaphoreType.DMA((count,)),
        ],
        compiler_params=pltpu.CompilerParams(vmem_limit_bytes=24 * MIB),
        cost_estimate=pl.CostEstimate(flops=40000000000, bytes_accessed=1 << 20, transcendentals=0),
        name="separator_part",
    )(*[in_hbm(value) for value in (loads, lower, weights, rows, right, inverse)])


def joined_blocks(before, lower, weights, rows, eliminated, turns):
    count, _, size, inner = weights.shape
    shots = eliminated.shape[1] // 2

    def kernel(lower_hbm, weight_hbm, rows_ref, eliminated_hbm, *refs):
        joined_hbm, plain_hbm, lower_ref, weight_ref, eliminated_ref, joined_ref, plain_ref, arrived, left = refs[-9:]
        halves = lax.div(lax.axis_index("slab"), GROUP) == turns - 2
        first = 0 if before is None else count // 2
        last = jnp.where(halves == (before is None), count // 2, count)

        def copies(b):
            sources = (lower_hbm, weight_hbm, eliminated_hbm)
            rooms = (lower_ref, weight_ref, eliminated_ref)
            slot = lax.rem(b, 2)
            return [
                pltpu.make_async_copy(source.at[b], room.at[slot], arrived.at[i, slot])
                for i, (source, room) in enumerate(zip(sources, rooms))
            ]

        def leaving(b):
            slot = lax.rem(b, 2)
            return [
                pltpu.make_async_copy(joined_ref.at[slot], joined_hbm.at[b], left.at[0, slot]),
                pltpu.make_async_copy(plain_ref.at[slot], plain_hbm.at[b], left.at[1, slot]),
            ]

        @pl.when(last > first)
        def _():
            for copy in copies(first):
                copy.start()

            @pl.loop(first, last)
            def _(b):
                slot = lax.rem(b, 2)

                @pl.when(b + 1 < last)
                def _():
                    for copy in copies(b + 1):
                        copy.start()

                @pl.when(b >= first + 2)
                def _():
                    for copy in leaving(b - 2):
                        copy.wait()

                for copy in copies(b):
                    copy.wait()
                joined = column_product(weight_ref.at[slot], side_by_side(lower_ref.at[slot]))
                joined = spread_product(spread_of(rows_ref[pl.ds(b, 1)]), joined)
                for half in range(2):
                    high, low = split(joined[:, half * inner : (half + 1) * inner])
                    joined_ref[slot, half, 0] = high
                    joined_ref[slot, half, 1] = low
                rows_now = split(eliminated_ref[slot])
                real = near_dot(rows_now, split(lower_ref[slot, 0]))
                imag = near_dot(rows_now, split(lower_ref[slot, 1]))
                plain_ref[slot, :shots] = real[:shots] - imag[shots:]
                plain_ref[slot, shots:] = real[shots:] + imag[:shots]
                for copy in leaving(b):
                    copy.start()

            @pl.loop(jnp.maximum(first, last - 2), last)
            def _(b):
                for copy in leaving(b):
                    copy.wait()

    hbm = pl.BlockSpec(memory_space=pltpu.HBM)
    operands = [in_hbm(lower), in_hbm(weights), rows, in_hbm(eliminated)]
    specs = [hbm, hbm, whole(), hbm]
    aliases = {}
    if before is not None:
        aliases = {4: 0, 5: 1}
        operands += [in_hbm(value) for value in before]
        specs += [hbm] * 2
    return pl.pallas_call(
        kernel,
        out_shape=(
            pltpu.HBM((count, 2, 2, size, inner), jnp.bfloat16),
            pltpu.HBM((count, 2 * shots, inner), jnp.float32),
        ),
        in_specs=specs,
        out_specs=(hbm, hbm),
        scratch_shapes=[
            pltpu.VMEM((2,) + lower.shape[1:], jnp.float32),
            pltpu.VMEM((2,) + weights.shape[1:], jnp.float32),
            pltpu.VMEM((2,) + eliminated.shape[1:], jnp.float32),
            pltpu.VMEM((2, 2, 2, size, inner), jnp.bfloat16),
            pltpu.VMEM((2, 2 * shots, inner), jnp.float32),
            pltpu.SemaphoreType.DMA((3, 2)),
            pltpu.SemaphoreType.DMA((2, 2)),
        ],
        input_output_aliases=aliases,
        compiler_params=pltpu.CompilerParams(vmem_limit_bytes=12 * MIB),
        cost_estimate=LIGHT,
        name="joined_blocks",
    )(*operands)


def finish(arrived, joined, plain):
    count, _, _, size, inner = joined.shape
    pieces, height, _ = arrived.shape
    subs = pieces // GROUP
    width = height // 2
    shots = pieces * width

    def kernel(arrived_ref, joined_ref, plain_ref, interior_hbm, solution_hbm, solved, interior, solution, left):
        for half in range(2):
            for sub in range(subs):
                for member in range(GROUP):
                    start = half * shots + (sub * GROUP + member) * width
                    solved[start : start + width] = arrived_ref[
                        member * subs + sub, half * width : (half + 1) * width
                    ]
        rows_now = split(solved[...])
        for half in range(2):
            solution[half] = solved[half * shots : (half + 1) * shots].T
        copies = [pltpu.make_async_copy(solution, solution_hbm, left.at[count])]
        copies[0].start()
        for block in range(count):
            real = near_dot(rows_now, (joined_ref[block, 0, 0], joined_ref[block, 0, 1]))
            imag = near_dot(rows_now, (joined_ref[block, 1, 0], joined_ref[block, 1, 1]))
            interior[block, 0] = (plain_ref[block, :shots] - (real[:shots] - imag[shots:])).T
            interior[block, 1] = (plain_ref[block, shots:] - (real[shots:] + imag[:shots])).T
            copies.append(
                pltpu.make_async_copy(interior.at[block], interior_hbm.at[block], left.at[block])
            )
            copies[-1].start()
        for copy in copies:
            copy.wait()

    hbm = pl.BlockSpec(memory_space=pltpu.HBM)
    return pl.pallas_call(
        kernel,
        out_shape=(
            pltpu.HBM((count, 2, inner, shots), jnp.float32),
            pltpu.HBM((2, size, shots), jnp.float32),
        ),
        in_specs=[whole()] * 3,
        out_specs=(hbm, hbm),
        scratch_shapes=[
            pltpu.VMEM((2 * shots, size), jnp.float32),
            pltpu.VMEM((count, 2, inner, shots), jnp.float32),
            pltpu.VMEM((2, size, shots), jnp.float32),
            pltpu.SemaphoreType.DMA((count + 1,)),
        ],
        compiler_params=pltpu.CompilerParams(vmem_limit_bytes=12 * MIB),
        name="finish",
    )(arrived, joined, plain)


def flip_blocks(blocks):
    size = blocks.shape[-1]

    def kernel(blocks_ref, out):
        @pl.when(lax.axis_index("slab") >= GROUP)
        def _():
            @pl.loop(0, 4 * GROUP)
            def _(i):
                slot, part, half = lax.div(i, 4), lax.rem(lax.div(i, 2), 2), lax.rem(i, 2)
                rows = pl.ds(pl.multiple_of(half * size, size), size)
                out[slot, part, rows] = blocks_ref[slot, part, rows].T

    return pl.pallas_call(
        kernel,
        out_shape=pltpu.VMEM(blocks.shape, blocks.dtype),
        in_specs=[whole()],
        out_specs=whole(),
        compiler_params=pltpu.CompilerParams(vmem_limit_bytes=12 * MIB),
        cost_estimate=LIGHT,
        name="flip_blocks",
    )(blocks)


def turn(state, answer, incoming, blocks, flipped, group, forward, backward):
    shape = state.shape[1:]
    subs = answer.shape[1]

    def kernel(*refs):
        state_in, _, block_ref = refs[:3]
        incoming_ref = None if incoming is None else refs[3]
        flipped_ref = None if flipped is None else refs[4]
        state_out, answer_out, _, carry = refs[-4:]
        position = lax.axis_index("slab")
        member = lax.rem(position, GROUP)

        @pl.when(lax.div(position, GROUP) == group)
        def _():
            value = None if incoming is None else incoming_ref[...]
            if forward:
                for i in range(GROUP):
                    slot = member ^ i
                    local = state_in[slot]
                    if value is None:
                        value = local
                    elif flipped is None:
                        value = local - row_product(value, block_ref, slot, dot_flipped)
                    else:
                        value = local - row_product(value, flipped_ref, slot, dot)
                    state_out[slot] = value
                carry[...] = value
            if backward:
                value = None if forward else value
                for i in reversed(range(GROUP)):
                    slot = member ^ i
                    trace = state_out[slot] if forward else state_in[slot]
                    value = trace if value is None else trace - value
                    for sub in range(subs):
                        answer_out[i, sub] = value
                    if i or group:
                        value = row_product(value, block_ref, slot, dot)
                carry[...] = value

    operands = (state, answer, blocks) + tuple(x for x in (incoming, flipped) if x is not None)
    return pl.pallas_call(
        kernel,
        out_shape=(
            jax.ShapeDtypeStruct(state.shape, jnp.float32),
            jax.ShapeDtypeStruct(answer.shape, jnp.float32),
            pltpu.VMEM(blocks.shape, blocks.dtype),
            jax.ShapeDtypeStruct(shape, jnp.float32),
        ),
        in_specs=[whole()] * len(operands),
        out_specs=(whole(),) * 4,
        input_output_aliases={0: 0, 1: 1, 2: 2},
        compiler_params=pltpu.CompilerParams(vmem_limit_bytes=16 * MIB),
        name="sweep_turn",
    )(*operands)


def body(
    rhs_interior,
    rhs_separator,
    inverse_blocks,
    coupling,
    separator_rows,
    separator_inverse,
    transfer,
):
    slabs, subs = lax.axis_size("slab"), lax.axis_size("sub")
    member = lax.rem(lax.axis_index("slab"), GROUP)
    turns = slabs // GROUP
    loads, lower, weights, rows = rhs_interior[0], inverse_blocks[0], coupling[0], separator_rows[0]
    groups = [
        [(g * GROUP + m) * subs + u for m in range(GROUP) for u in range(subs)] for g in range(turns)
    ]

    def exchange(value):
        return lax.all_to_all(value, ("slab", "sub"), 0, 0, axis_index_groups=groups, tiled=True)

    own = transfer[0].reshape(-1, transfer.shape[-1])
    crossed, near = crossed_blocks(own, swap(own, 1))
    near, rows = lax.optimization_barrier((near, rows))
    terms, eliminated = separator_part(
        loads, lower, weights, rows, rhs_separator[0], separator_inverse[0]
    )
    crossed[:RELAYED], terms = lax.optimization_barrier((crossed[:RELAYED], terms))
    pieces = [piece for c in range(RELAYED) for piece in relayed_pieces(c, crossed[c])]
    pieces += [(c, 0, crossed[c]) for c in range(RELAYED, RELAYED + DIRECT)]
    terms = exchange(terms)
    early = [swap(piece, 1) if k == 0 and c < RELAYED else None for c, k, piece in pieces]
    settled, terms = lax.optimization_barrier(([piece for _, _, piece in pieces], terms))
    pieces = [(c, k, piece) for (c, k, _), piece in zip(pieces, settled)]
    far = [swap(piece, 1) if sent is None else sent for piece, sent in zip(settled, early)]
    blocks, state = split_blocks(own, near, pieces, terms)
    blocks = split_last(blocks, pieces, far)

    def hop(value, source, steps):
        return move(
            value,
            lambda slab, sub: (slab + GROUP * steps, sub) if slab // GROUP == source else None,
        )

    incoming = joined = flipped = None
    answer = jnp.zeros((GROUP, subs) + state.shape[1:], jnp.float32)
    for group in range(turns):
        last = group == turns - 1
        state, answer, blocks, carry = turn(
            state, answer, incoming, blocks, flipped, group, True, last
        )
        if not last:
            incoming = hop(carry, group, 1)
        if not group:
            state, blocks = lax.optimization_barrier((state, blocks))
            flipped = flip_blocks(blocks)
    for group in reversed(range(turns - 1)):
        incoming = hop(carry, group + 1, -1)
        if group >= turns - 3:
            carry, eliminated = lax.optimization_barrier((carry, eliminated))
            joined = joined_blocks(joined, lower, weights, rows, eliminated, turns)
            state, joined = lax.optimization_barrier((state, joined))
        state, answer, blocks, carry = turn(
            state, answer, incoming, blocks, None, group, False, True
        )

    arrived = exchange(answer.reshape((GROUP * subs,) + answer.shape[2:]))
    interior, solved = finish(arrived, *joined)
    return (interior[None], solved[None])


def solution(mesh):
    in_specs = (
        P("slab", "sub", None, None, None),
        P("slab", None, None, None),
        P("slab", "sub", None, None, None),
        P("slab", "sub", None, None, None),
        P("slab", "sub", None),
        P("slab", None, None, None),
        P("slab", None, None, None),
    )
    out_specs = (P("slab", "sub", None, None, None), P("slab", None, None, None))
    return jax.shard_map(body, mesh=mesh, in_specs=in_specs, out_specs=out_specs, check_vma=False)
```
